512 devices in a mesh: ens: 8 (over z_hi, core), space: 64 (over z_lo, y, x).
Axes of the slice: x: 4, y: 4, z: 16 (z_hi: 4, z_lo: 4; z = z_hi * 4 + z_lo), core: 2. Of those that a mesh axis runs over, the one named last changes fastest.
Arguments:
- latents: bfloat16 [16, 8192, 1024], P('ens', 'space'), may hold values from -16 to 16
- queries: bfloat16 [16, 8192, 1024], P('ens', 'space'), may hold values from -192 to 192
- attn_keys: bfloat16 [16, 8192, 1024], P('ens', 'space'), may hold values from -6 to 6
- value_weight: bfloat16 [1024, 1024], P('space'), may hold values from -0.1875 to 0.1875
- decoder: bfloat16 [1024, 100], replicated, may hold values from -0.1875 to 0.1875
- targets: float32 [100, 8192], P(None, 'space'), may hold values from -8 to 8
- send_rows: int32 [2, 2048], P(None, 'space'), may hold values from 0 to 127, as said below
- neighbours: int32 [8192, 16], P('space'), may hold values from 0 to 191, as said below
- live_slots: int32 [8192], P('space'), may hold values from 8 to 16, as said below
- loss_multiplier: float32 [1], replicated, may hold values from 1 to 4
Outputs:
- loss_value: float32 [1], replicated
- grad_latents: bfloat16 [16, 8192, 1024], P('ens', 'space')
- grad_queries: bfloat16 [16, 8192, 1024], P('ens', 'space')
- grad_keys: bfloat16 [16, 8192, 1024], P('ens', 'space')
- grad_weight: float32 [1024, 1024], P('space')
The draws below stay inside these ranges and needn't reach their ends.
Inputs may be any that keep to these rules, and one draw needn't show every extreme that they name: `send_rows`: row 0 of a shard's block lists 32 of its own rows, from the first half of the shard, read by the shard before it along space (wrapping); row 1 lists 32 rows from the second half, read by the shard after it. Repeats may occur. `neighbours`: entry [n, t] indexes the wide rows of n's shard: the 32 rows received from the shard before it in the order of its list, the shard's own 128 rows, then the 32 rows received from the shard after it. Slot 0 is the node itself. Repeats may occur and then count twice. Node n uses its first live_slots[n] slots.
All inputs are finite; a program needn't handle non-finite values.
Results may differ from the reference program's by a relative error of at most 0.015.
Values may be sent and summed in bfloat16 or wider, within the bound.
A program may use at most 128 MiB of HBM per device.

```python
import math
import jax
import jax.numpy as jnp
from jax import lax

D = 1024
HEADS = 16
OUTPUT_CHANNELS = 100
ENSEMBLE_COUNT = 16
ROWS = 128
HALO = 32
NBR = 16
GRID_NODES = 8192
N_SPACE = 64


def shared_keys(key):
    return jnp.clip(jax.random.normal(jax.random.fold_in(key, 100), (ENSEMBLE_COUNT, GRID_NODES, D), jnp.float32), -6.0, 6.0)


def draw_attn_keys(key, part):
    base_keys = shared_keys(key)
    return base_keys.astype(jnp.bfloat16)


def draw_queries(key, part):
    key = jax.random.fold_in(key, 22)
    fresh = jnp.clip(jax.random.normal(key, (ENSEMBLE_COUNT, GRID_NODES, D), jnp.float32), -6.0, 6.0)
    return fresh.astype(jnp.bfloat16)


def draw_send_rows(key, part):
    key = jax.random.fold_in(key, 31)
    device_count = GRID_NODES // ROWS
    first_key, second_key = jax.random.split(key)
    lower_rows = jax.random.randint(first_key, (device_count, HALO), 0, ROWS // 2, dtype=jnp.int32)
    upper_rows = jax.random.randint(second_key, (device_count, HALO), ROWS // 2, ROWS, dtype=jnp.int32)
    lower_rows = lower_rows.at[:, 0].set(0)
    upper_rows = upper_rows.at[:, HALO - 1].set(ROWS - 1)
    return jnp.stack([lower_rows.reshape(-1), upper_rows.reshape(-1)], axis=0).astype(jnp.int32)


def draw_neighbours(key, part):
    key = jax.random.fold_in(key, 41)
    extent = ROWS + 2 * HALO
    picks = jax.random.randint(key, (GRID_NODES, NBR), 0, extent, dtype=jnp.int32)
    local_ids = jnp.arange(GRID_NODES, dtype=jnp.int32) % ROWS
    leading = local_ids == 0
    picks = picks.at[:, 0].set(HALO + local_ids)
    picks = picks.at[:, 1].set(jnp.where(leading, extent - 1, picks[:, 1]))
    picks = picks.at[:, 2].set(jnp.where(leading, 0, picks[:, 2]))
    return picks.astype(jnp.int32)


def draw_live_slots(key, part):
    key = jax.random.fold_in(key, 51)
    counts = jax.random.randint(key, (GRID_NODES,), NBR // 2, NBR + 1, dtype=jnp.int32)
    local_ids = jnp.arange(GRID_NODES, dtype=jnp.int32) % ROWS
    counts = jnp.where(local_ids == 0, NBR, counts)
    counts = jnp.where(local_ids == 1, NBR // 2, counts)
    return counts.astype(jnp.int32)


def with_spikes(array, key, source, target, parts, factor):
    owner, partner = [(jnp.arange(array.shape[dim]) // (array.shape[dim] // parts)).reshape([-1 if axis == dim else 1 for axis in range(array.ndim)]) for dim in (source, target)]
    chosen = jax.random.permutation(key, parts)[partner]
    strong = (owner == chosen) | (owner == (partner + parts // 2) % parts)
    return jnp.where(strong, factor * array, array)


def shard_levels(own_key, dims, cuts, low, top_value):
    gain = 1.0
    for dim, shards_of in cuts:
        heights = jax.random.uniform(jax.random.fold_in(jax.random.fold_in(own_key, 6), dim), (shards_of,), jnp.float32, low / len(cuts), top_value / len(cuts))
        gain = gain * jnp.repeat(jnp.exp(heights), dims[dim] // shards_of).reshape((-1,) + (1,) * (len(dims) - 1 - dim))
    return gain


def noise(rng, dims, scale, reach, pieces=(), held_as=jnp.bfloat16):
    array = scale * jax.random.normal(rng, dims, jnp.float32)
    if pieces:
        array = array * shard_levels(rng, dims, pieces, -0.22, 0.18)
    return jnp.clip(array, -reach, reach).astype(held_as)


def bell_draw_with(key, shape, scale, bound, cuts, heavy, kind=jnp.bfloat16):
    drawn = scale * jax.random.normal(key, shape, jnp.float32)
    if cuts:
        drawn = drawn * shard_levels(key, shape, cuts, -0.22, 0.18)
    return jnp.clip(with_spikes(drawn, jax.random.fold_in(key, 3), *heavy), -bound, bound).astype(kind)


def setup_inputs(seed: int = 0) -> dict:
    streams_of = jax.random.split(jax.random.key(seed), 11)
    return {
        "latents": bell_draw_with(streams_of[0], (ENSEMBLE_COUNT, GRID_NODES, D), 1.0, 16.0, ((0, 8), (1, 64)), (1, 2, 64, 4.0)),
        "queries": draw_queries(jax.random.fold_in(streams_of[10], 71), 0),
        "attn_keys": draw_attn_keys(jax.random.fold_in(streams_of[10], 71), 0),
        "value_weight": noise(streams_of[3], (D, D), D ** -0.5, 0.1875, ((0, 64),)),
        "decoder": noise(streams_of[4], (D, OUTPUT_CHANNELS), D ** -0.5, 0.1875),
        "targets": noise(streams_of[5], (OUTPUT_CHANNELS, GRID_NODES), 1.5, 8.0, ((1, 64),), jnp.float32),
        "send_rows": draw_send_rows(jax.random.fold_in(streams_of[10], 71), 0),
        "neighbours": draw_neighbours(jax.random.fold_in(streams_of[10], 71), 0),
        "live_slots": draw_live_slots(jax.random.fold_in(streams_of[10], 71), 0),
        "loss_multiplier": jnp.clip(jnp.exp(jax.random.uniform(streams_of[9], (1,), jnp.float32, math.log(1.0), math.log(4.0))), 1.0, 4.0),
    }


smooth = 0.1

def linkage(neighbour_ids, live_count, extent):
    slot_ids = jnp.arange(neighbour_ids.shape[1], dtype=jnp.int32)
    in_use = (slot_ids[None, :] < live_count[:, None]).astype(jnp.float32)
    target_ids = jnp.arange(extent, dtype=jnp.int32)
    matches = (neighbour_ids[:, :, None] == target_ids[None, None, :]).astype(jnp.float32)
    return lax.optimization_barrier(jnp.sum(in_use[:, :, None] * matches, axis=1))

def attend(value_inputs, key_rows, query_rows, latent_rows, linkage_map, decoder):
    ensemble_members, row_count, width = query_rows.shape
    extent = key_rows.shape[1]
    head_size = width // HEADS
    query_half = query_rows.astype(jnp.bfloat16).astype(jnp.float32).reshape(ensemble_members, row_count, HEADS, head_size)
    key_half = key_rows.astype(jnp.bfloat16).astype(jnp.float32).reshape(ensemble_members, extent, HEADS, head_size)
    value_half = value_inputs.astype(jnp.bfloat16).astype(jnp.float32).reshape(ensemble_members, extent, HEADS, head_size)
    scores = jnp.einsum('mrhc,mjhc->mhrj', query_half, key_half) * head_size ** (-0.5)
    masked = jnp.where(linkage_map[None, None] > 0, scores, -1e+30)
    largest = lax.optimization_barrier(jnp.max(masked, axis=-1, keepdims=True))
    raised = linkage_map[None, None] * jnp.exp(masked - largest)
    attn_weight = (raised / lax.optimization_barrier(jnp.sum(raised, axis=-1, keepdims=True))).astype(jnp.bfloat16)
    mixed = jnp.einsum('mhrj,mjhc->mrhc', attn_weight.astype(jnp.float32), value_half).reshape(ensemble_members, row_count, width)
    output_rows = (latent_rows + mixed).astype(jnp.bfloat16)
    return jnp.einsum('mrd,dc->mcr', output_rows.astype(jnp.float32), decoder.astype(jnp.float32))

def score_parts(prediction, observation, weighting):
    ensemble_members = prediction.shape[0]
    member_shift = prediction - observation[None]
    spread = jnp.sqrt(member_shift * member_shift + smooth * smooth)
    pair_total = jnp.zeros(observation.shape, jnp.float32)
    pairwise_slope = jnp.zeros(prediction.shape, jnp.float32)
    for member_index in range(ensemble_members):
        pairwise_distance = prediction - prediction[member_index][None]
        radius = jnp.sqrt(pairwise_distance * pairwise_distance + smooth * smooth)
        pair_total = pair_total + lax.optimization_barrier(jnp.sum(radius - smooth, axis=0))
        pairwise_slope = pairwise_slope + pairwise_distance / radius
    score_terms = lax.optimization_barrier(jnp.mean(spread - smooth, axis=0)) - pair_total / (2.0 * ensemble_members * (ensemble_members - 1))
    score_slope = weighting * (member_shift / spread / ensemble_members - pairwise_slope / (ensemble_members * (ensemble_members - 1)))
    return (score_slope, score_terms)

def reference(latents, queries, attn_keys, value_weight, decoder, targets, send_rows, neighbours, live_slots, loss_multiplier):
    extent = ROWS + 2 * HALO
    shard_indices = jnp.arange(N_SPACE, dtype=jnp.int32)
    weight_full = value_weight.astype(jnp.float32)

    def shard_rows(source, index):
        return lax.dynamic_slice_in_dim(source, index * ROWS, ROWS, 1)

    def send_block(index):
        return lax.dynamic_slice_in_dim(send_rows, index * HALO, HALO, 1)

    def neighbours_of(index):
        left_dev = (index + N_SPACE - 1) % N_SPACE
        right_dev = (index + 1) % N_SPACE
        return (left_dev, right_dev)

    def extend(source, index):
        left_dev, right_dev = neighbours_of(index)
        return jnp.concatenate([jnp.take(shard_rows(source, left_dev), send_block(left_dev)[1], axis=1), shard_rows(source, index), jnp.take(shard_rows(source, right_dev), send_block(right_dev)[0], axis=1)], axis=1)

    def shard_inputs(index):
        wide_latents = extend(latents, index)
        broad_keys = extend(attn_keys, index).astype(jnp.float32)
        neighbour_ids = lax.dynamic_slice_in_dim(neighbours, index * ROWS, ROWS, 0)
        live_count = lax.dynamic_slice_in_dim(live_slots, index * ROWS, ROWS, 0)
        linkage_map = linkage(neighbour_ids, live_count, extent)
        value_inputs = jnp.einsum('mjd,de->mje', wide_latents.astype(jnp.float32), weight_full)
        return (wide_latents, broad_keys, shard_rows(queries, index).astype(jnp.float32), shard_rows(latents, index).astype(jnp.float32), linkage_map, value_inputs)

    def forward_apply(index):
        wide_latents, broad_keys, query_rows, latent_rows, linkage_map, value_inputs = shard_inputs(index)
        return attend(value_inputs, broad_keys, query_rows, latent_rows, linkage_map, decoder)
    predictions = lax.map(forward_apply, shard_indices)
    prediction = jnp.transpose(predictions, (1, 2, 0, 3)).reshape(ENSEMBLE_COUNT, OUTPUT_CHANNELS, GRID_NODES)
    score_slope, score_terms = score_parts(prediction, targets, loss_multiplier[0])
    loss_value = (jnp.sum(score_terms) / (GRID_NODES * OUTPUT_CHANNELS)).reshape(1)

    def backward(running, index):
        grad_lat, grad_key, grad_wt = running
        wide_latents, broad_keys, query_rows, latent_rows, linkage_map, value_inputs = shard_inputs(index)
        slope_block = lax.dynamic_slice_in_dim(score_slope, index * ROWS, ROWS, 2)

        def local_forward(value_in, key_in, query_in, latent_in):
            return attend(value_in, key_in, query_in, latent_in, linkage_map, decoder)
        unused, pullback = jax.vjp(local_forward, value_inputs, broad_keys, query_rows, latent_rows)
        grad_values, grad_wkeys, grad_query, grad_resid = pullback(slope_block)
        grad_wide = jnp.einsum('mje,de->mjd', grad_values, weight_full)
        grad_wt = grad_wt + jnp.einsum('mjd,mje->de', wide_latents.astype(jnp.float32), grad_values)
        left_dev, right_dev = neighbours_of(index)
        rows_left = left_dev * ROWS + send_block(left_dev)[1]
        rows_right = right_dev * ROWS + send_block(right_dev)[0]
        rows_own = index * ROWS + jnp.arange(ROWS, dtype=jnp.int32)
        grad_lat = grad_lat.at[:, rows_left].add(grad_wide[:, :HALO])
        grad_lat = grad_lat.at[:, rows_own].add(grad_wide[:, HALO:HALO + ROWS] + grad_resid)
        grad_lat = grad_lat.at[:, rows_right].add(grad_wide[:, HALO + ROWS:])
        grad_key = grad_key.at[:, rows_left].add(grad_wkeys[:, :HALO])
        grad_key = grad_key.at[:, rows_own].add(grad_wkeys[:, HALO:HALO + ROWS])
        grad_key = grad_key.at[:, rows_right].add(grad_wkeys[:, HALO + ROWS:])
        return ((grad_lat, grad_key, grad_wt), grad_query.astype(jnp.bfloat16))
    start_state = (jnp.zeros((ENSEMBLE_COUNT, GRID_NODES, D), jnp.float32), jnp.zeros((ENSEMBLE_COUNT, GRID_NODES, D), jnp.float32), jnp.zeros((D, D), jnp.float32))
    final_state, query_parts = lax.scan(backward, start_state, shard_indices)
    grad_lat, grad_key, grad_wt = final_state
    grad_queries = jnp.transpose(query_parts, (1, 0, 2, 3)).reshape(ENSEMBLE_COUNT, GRID_NODES, D)
    return (loss_value, grad_lat.astype(jnp.bfloat16), grad_queries, grad_key.astype(jnp.bfloat16), grad_wt)
```

```python
import jax
import jax.numpy as jnp
from jax import lax
from jax.experimental import pallas as pl
from jax.experimental.pallas import tpu as pltpu
from jax.sharding import PartitionSpec as P

MESH = pl.DeviceIdType.MESH
F32 = jnp.float32
BF16 = jnp.bfloat16
M, R, D, H, W = 2, 128, 1024, 32, 192
PAIRS = 8
CH = 13
MEMBERS = 16
CHANNELS = 100
SMOOTH = 0.1
NT = (((1,), (1,)), ((), ()))
TN = (((0,), (0,)), ((), ()))


def dot(a, b, dims=(((1,), (0,)), ((), ()))):
    return lax.dot_general(a, b, dims, preferred_element_type=F32)


def iota(shape, dim):
    return lax.broadcasted_iota(jnp.int32, shape, dim)


def kernel(
    L, Q, K, wsh, dec, tgt, srows, nbr, live, mult,
    o_loss, o_dl, o_dq, o_dk, o_dw,
    wg, wf, wl, kw, qt, lt, wlt, lk, oneh, snd_l, snd_k,
    decp, decpt, tgo, pf, pb, vv, outt, fs, fa, sl, sr, dot_t, dv, dk, rv, rk,
    e1s, e1r, s1, r1, a2, s2, r2, a3, s3, r3, s4, r4, fin, lsend, lrecv,
    ssem, rsem,
):
    e = lax.axis_index("ens")
    s = lax.axis_index("space")
    zh, c = e // 2, e % 2
    zl, y, x = s // 16, (s // 4) % 4, s % 4
    a = y * (1 - c) + x * c
    b = x * (1 - c) + y * c
    b_other = y * (1 - c) + x * c

    def at(e_, zl_, y_, x_):
        return (e_, zl_ * 16 + y_ * 4 + x_)

    sibling = (zh * 2 + 1 - c, s)

    def peer_a(k):
        return at(e, zl, (y + k * (1 - c)) % 4, (x + k * c) % 4)

    def peer_b(k):
        return at(e, zl, (y + k * c) % 4, (x + k * (1 - c)) % 4)

    def peer_zl(k):
        return at(e, (zl + k) % 4, y, x)

    def peer_zh(k):
        return (((zh + k) % 4) * 2 + c, s)

    def peer_ens(k):
        return ((e + k) % 8, s)

    right = (e, (s + 1) % 64)
    left = (e, (s + 63) % 64)

    barrier = pltpu.get_barrier_semaphore()
    partners = [peer_a(k) for k in (1, 2, 3)] + [peer_b(k) for k in (1, 2, 3)]
    partners += [peer_zl(k) for k in (1, 2, 3)] + [peer_ens(k) for k in range(1, 8)]
    partners += [right, left]
    for p in partners:
        pl.semaphore_signal(barrier, inc=1, device_id=p, device_id_type=MESH)

    sent = []
    count = [0]

    def send(src, dst, device):
        k = count[0]
        count[0] += 1
        copy = pltpu.make_async_remote_copy(
            src_ref=src, dst_ref=dst, send_sem=ssem.at[k], recv_sem=rsem.at[k],
            device_id=device, device_id_type=MESH,
        )
        copy.start()
        sent.append(copy)
        return copy

    rows = iota((R, H), 0)
    to_right = (rows == srows[1:2, :]).astype(F32).astype(BF16)
    to_left = (rows == srows[0:1, :]).astype(F32).astype(BF16)
    oneh[:, 0:H] = to_right
    oneh[:, H:2 * H] = to_left
    for m in range(M):
        snd_k[0, m] = dot(to_right, K[m], TN).astype(BF16)
        snd_k[1, m] = dot(to_left, K[m], TN).astype(BF16)
        snd_l[0, m] = dot(to_right, L[m], TN).astype(BF16)
        snd_l[1, m] = dot(to_left, L[m], TN).astype(BF16)
    wg[c, b, zl, a] = wsh[:, pl.ds(pl.multiple_of(c * 512, 512), 512)]

    pl.semaphore_wait(barrier, len(partners))

    w1 = [send(wg.at[c, b, zl, a], wg.at[c, b, zl, a], peer_zl(k)) for k in (1, 2, 3)]
    hk = [
        send(snd_k.at[0], kw.at[:, pl.ds(R, H)], right),
        send(snd_k.at[1], kw.at[:, pl.ds(R + H, H)], left),
    ]

    for m in range(M):
        wl[m, 0:R] = L[m]
        kw[m, 0:R] = K[m]
    node_ids = dot((iota((16, 16), 0) == iota((16, 16), 1)).astype(F32).astype(BF16),
                   nbr[...].astype(F32).astype(BF16), NT)
    row = iota((W, R), 0)
    wide_id = jnp.where(row < R, row + H, jnp.where(row < R + H, row - R, row)).astype(F32)
    used = live[...]
    links = jnp.zeros((W, R), F32)
    for t in range(16):
        hit = jnp.where(used > t, node_ids[t:t + 1, :], -1.0) == wide_id
        links = links + jnp.where(hit, 1.0, 0.0)
    lk[:, 0:R] = links
    lk[:, R:2 * R] = links

    for k in range(3):
        w1[k].wait_recv()
    w2 = [send(wg.at[c, b, :, a], wg.at[c, b, :, a], peer_a(k)) for k in (1, 2, 3)]
    hl = [
        send(snd_l.at[0], wl.at[:, pl.ds(R, H)], right),
        send(snd_l.at[1], wl.at[:, pl.ds(R + H, H)], left),
    ]

    for m in range(M):
        for d in range(8):
            qt[m, d * 128:(d + 1) * 128, :] = Q[m, :, d * 128:(d + 1) * 128].T
            lt[m, d * 128:(d + 1) * 128, :] = L[m, :, d * 128:(d + 1) * 128].T
    slot, chan = iota((128, CHANNELS), 0), iota((128, CHANNELS), 1)
    place = ((slot % 16 < CH) & (chan == (slot // 16) * CH + slot % 16)).astype(F32).astype(BF16)
    decp[...] = dot(dec[...], place, NT).astype(BF16)
    decpt[...] = dot(place, dec[...], NT).astype(BF16)
    slot16, chan16 = iota((16, CHANNELS), 0), iota((16, CHANNELS), 1)
    own_place = ((slot16 < CH) & (chan16 == e * CH + slot16)).astype(F32)
    tgo[...] = lax.dot_general(
        own_place, tgt[...], (((1,), (0,)), ((), ())),
        precision=lax.Precision.HIGHEST, preferred_element_type=F32,
    )

    for k in range(3):
        w2[k].wait_recv()
    w3 = [send(wg.at[c, b], wg.at[c, b], peer_b(k)) for k in (1, 2, 3)]
    wd = [send(wg.at[c, b], wg.at[c, b], sibling)]

    for k in range(2):
        hk[k].wait_recv()

    top = iota((128, R), 0) < 64

    def spread(block):
        zero = jnp.zeros_like(block)
        return jnp.concatenate([jnp.where(top, block, zero), jnp.where(top, zero, block)], axis=1)

    def folded(block):
        return jnp.where(top, block[:, 0:R], block[:, R:2 * R])

    def cols(p):
        return pl.ds(pl.multiple_of(p * 128, 128), 128)

    def weights_of(p, _):
        link = lk[...]
        for m in range(M):
            scores = dot(kw[m, :, cols(p)], spread(qt[m, cols(p), :])) * 0.125
            masked = jnp.where(link > 0, scores, -1e30)
            raised = link * jnp.exp(masked - jnp.max(masked, axis=0, keepdims=True))
            weight = raised * (1.0 / jnp.sum(raised, axis=0, keepdims=True))
            pf[m, p] = weight
            pb[m, p] = weight.astype(BF16)
        return 0

    lax.fori_loop(0, 4, weights_of, 0)
    for k in range(3):
        w3[k].wait_recv()
        bk = (b + 3 - k) % 4
        wd.append(send(wg.at[c, bk], wg.at[c, bk], sibling))
    lax.fori_loop(4, PAIRS, weights_of, 0)
    for k in range(2):
        hl[k].wait_recv()
    for k in range(4):
        wd[k].wait_recv()

    for z_ in range(4):
        for y_ in range(4):
            for x_ in range(4):
                d = z_ * 256 + y_ * 64 + x_ * 16
                wf[d:d + 16, 0:512] = wg[0, x_, z_, y_]
                wf[d:d + 16, 512:1024] = wg[1, y_, z_, x_]

    def mix(m):
        def step(p, _):
            mixed = folded(dot(vv[m, :, cols(p)], pb[m, p], TN))
            outt[m, cols(p), :] = (lt[m, cols(p), :].astype(F32) + mixed).astype(BF16)
            return 0
        return step

    def values_of(m):
        def step(q, _):
            block = pl.ds(pl.multiple_of(q * 256, 256), 256)
            vv[m, :, block] = dot(wl[m], wf[:, block]).astype(BF16)
            return 0
        return step

    fx = []
    for m in range(M):
        lax.fori_loop(0, 4, values_of(m), 0)
        lax.fori_loop(0, PAIRS, mix(m), 0)
        fs[m] = dot(decpt[...], outt[m]).reshape(8, 16, R)
        fa[2 * e + m] = fs[m, e]
        for k in range(1, 8):
            fx.append(send(fs.at[m, (e + k) % 8], fa.at[2 * e + m], peer_ens(k)))

    for m in range(M):
        for d in range(8):
            halo_t = wl[m, R:W, d * 128:(d + 1) * 128].T
            own_t = lt[m, d * 128:(d + 1) * 128, :]
            for i in range(8):
                g = d * 8 + i
                z_, y_, x_ = g // 16, (g // 4) % 4, g % 4
                r0 = (x_ * 16 + z_ * 4 + y_) * 16
                r1_ = (y_ * 16 + z_ * 4 + x_) * 16
                for h, r_ in ((0, r0), (1, r1_)):
                    wlt[h, m, r_:r_ + 16, 0:R] = own_t[i * 16:(i + 1) * 16]
                    wlt[h, m, r_:r_ + 16, R:W] = halo_t[i * 16:(i + 1) * 16]

    for copy in fx:
        copy.wait_recv()

    f = fa[...]
    shift = f - tgo[...][None]
    square = shift * shift + SMOOTH * SMOOTH
    inverse = lax.rsqrt(square)
    near = jnp.sum(square * inverse - SMOOTH, axis=0)
    pair_slope = jnp.zeros((MEMBERS, 16, R), F32)
    pair_total = jnp.zeros((16, R), F32)
    for k in range(1, 9):
        other = jnp.concatenate([f[k:], f[:k]], axis=0)
        gap = f - other
        sq = gap * gap + SMOOTH * SMOOTH
        inv = lax.rsqrt(sq)
        radius = sq * inv - SMOOTH
        slope = gap * inv
        if k < 8:
            pair_total = pair_total + jnp.sum(radius, axis=0)
            pair_slope = pair_slope + slope - jnp.concatenate([slope[MEMBERS - k:], slope[:MEMBERS - k]], axis=0)
        else:
            pair_total = pair_total + jnp.sum(radius[:8], axis=0)
            pair_slope = pair_slope + slope
    pair_norm = 1.0 / (MEMBERS * (MEMBERS - 1))
    sl[...] = (mult[0] * (shift * inverse * (1.0 / MEMBERS) - pair_slope * pair_norm)).astype(BF16)
    slot_id = iota((16, R), 0)
    real = (slot_id < CH) & (slot_id + e * CH < CHANNELS)
    terms = jnp.where(real, near * (1.0 / MEMBERS) - pair_total * pair_norm, 0.0)
    sr[e] = sl[pl.ds(2 * e, 2)]
    sx = [
        send(sl.at[pl.ds(2 * ((e + k) % 8), 2)], sr.at[e], peer_ens(k))
        for k in range(1, 8)
    ]
    lsend[0] = terms[0:8] + terms[8:16]
    l0 = send(lsend.at[0], lrecv.at[0, 0], sibling)
    for copy in sx:
        copy.wait_recv()

    for m in range(M):
        dot_t[m] = dot(decp[...], sr[:, m].reshape(128, R)).astype(BF16)

    def value_grads(half):
        def step(q, _):
            p = half * 4 + q
            for m in range(M):
                dv[half, m, :, cols(q)] = dot(pb[m, p], spread(dot_t[m, cols(p), :]), NT).astype(BF16)
            return 0
        lax.fori_loop(0, 4, step, 0)

    def weight_grad(half, block):
        block_rows = pl.ds(pl.multiple_of(block * 256, 256), 256)
        return dot(wlt[half, 0, block_rows, :], dv[half, 0]) + dot(wlt[half, 1, block_rows, :], dv[half, 1])

    value_grads(1 - c)
    x1 = []
    for k in (1, 2, 3, 0):
        block = (b_other + k) % 4
        e1s[k] = weight_grad(1 - c, block).astype(BF16)
        x1.append(send(e1s.at[k], e1r.at[k], sibling))
    value_grads(c)
    hv = [
        send(dv.at[:, :, pl.ds(R + H, H)], rv.at[:, :, pl.ds(H, H)], right),
        send(dv.at[:, :, pl.ds(R, H)], rv.at[:, :, pl.ds(0, H)], left),
    ]
    l0.wait_recv()
    lsend[1] = lsend[0] + lrecv[0, 0]
    lrecv[1, b] = lsend[1]
    x2 = []
    l1 = [send(lsend.at[1], lrecv.at[1, b], peer_b(k)) for k in (1, 2, 3)]
    for i, k in enumerate((1, 2, 3, 0)):
        total = weight_grad(c, (b + k) % 4)
        x1[i].wait_recv()
        total = total + e1r[k].astype(F32)
        if k:
            s1[k - 1] = total.astype(BF16)
            x2.append(send(s1.at[k - 1], r1.at[k - 1], peer_b(k)))
        else:
            a2[...] = total.reshape(4, 4, 16, 512)

    def attention_grads(p, _):
        for m in range(M):
            grad_weight = dot(vv[m, :, cols(p)], spread(dot_t[m, cols(p), :])).astype(BF16).astype(F32)
            weight = pf[m, p]
            drift = jnp.sum(grad_weight * weight, axis=0, keepdims=True)
            grad_scores = (weight * (grad_weight - drift) * 0.125).astype(BF16)
            dk[m, :, cols(p)] = dot(grad_scores, spread(qt[m, cols(p), :]), NT).astype(BF16)
            grad_q = folded(dot(kw[m, :, cols(p)], grad_scores, TN))
            o_dq[m, :, cols(p)] = grad_q.astype(BF16).T
        return 0

    lax.fori_loop(0, PAIRS, attention_grads, 0)
    hkb = [
        send(dk.at[:, pl.ds(R + H, H)], rk.at[:, pl.ds(H, H)], right),
        send(dk.at[:, pl.ds(R, H)], rk.at[:, pl.ds(0, H)], left),
    ]

    def loss_step(stage, copies, mine, peers):
        for copy in copies:
            copy.wait_recv()
        got = lrecv[stage]
        lsend[stage + 1] = (got[0] + got[1]) + (got[2] + got[3])
        if peers is None:
            return None
        lrecv[stage + 1, mine] = lsend[stage + 1]
        return [send(lsend.at[stage + 1], lrecv.at[stage + 1, mine], p) for p in peers]

    for k in range(3):
        x2[k].wait_recv()
    a2[...] = a2[...] + (
        r1[0].astype(F32) + r1[1].astype(F32) + r1[2].astype(F32)
    ).reshape(4, 4, 16, 512)
    x3 = []
    for k in (1, 2, 3):
        s2[k - 1] = a2[:, (a + k) % 4].astype(BF16)
        x3.append(send(s2.at[k - 1], r2.at[k - 1], peer_a(k)))
    l2 = loss_step(1, l1, a, [peer_a(k) for k in (1, 2, 3)])

    for copy in hv:
        copy.wait_recv()
    for m in range(M):
        parts = [
            (dv[h, m, 0:R].astype(F32) + dot(oneh[...], rv[h, m])).astype(BF16) for h in range(2)
        ]
        out = dot(sr[:, m].reshape(128, R), decpt[...], TN).astype(BF16).astype(F32)
        out = out + dot(parts[0], wf[:, 0:512], NT) + dot(parts[1], wf[:, 512:1024], NT)
        o_dl[m] = out.astype(BF16)

    for k in range(3):
        x3[k].wait_recv()
    a3[...] = a2[:, a] + (r2[0].astype(F32) + r2[1].astype(F32) + r2[2].astype(F32))
    x4 = []
    for k in (1, 2, 3):
        s3[k - 1] = a3[(zl + k) % 4].astype(BF16)
        x4.append(send(s3.at[k - 1], r3.at[k - 1], peer_zl(k)))
    l3 = loss_step(2, l2, zl, [peer_zl(k) for k in (1, 2, 3)])

    for copy in hkb:
        copy.wait_recv()
    for m in range(M):
        o_dk[m] = (dk[m, 0:R].astype(F32) + dot(oneh[...], rk[m])).astype(BF16)

    for k in range(3):
        x4[k].wait_recv()
    s4[...] = (a3[zl] + (r3[0].astype(F32) + r3[1].astype(F32) + r3[2].astype(F32))).astype(BF16)
    r4[zh] = s4[...]
    x5 = [send(s4, r4.at[zh], peer_zh(k)) for k in (1, 2, 3)]
    l4 = loss_step(3, l3, zh, [peer_zh(k) for k in (1, 2, 3)])
    for k in range(3):
        x5[k].wait_recv()
    fin[c] = (r4[0].astype(F32) + r4[1].astype(F32)) + (r4[2].astype(F32) + r4[3].astype(F32))
    x6 = send(fin.at[c], fin.at[c], sibling)
    loss_step(4, l4, None, None)
    lrecv[5, c] = lsend[5]
    l5 = send(lsend.at[5], lrecv.at[5, c], sibling)
    x6.wait_recv()
    o_dw[:, 0:512] = fin[0]
    o_dw[:, 512:1024] = fin[1]
    l5.wait_recv()
    o_loss[0, 0] = jnp.sum(lrecv[5, 0]) * (1.0 / (8192 * CHANNELS))
    for copy in sent:
        copy.wait_send()


N_COPIES = 96


def body(latents, queries, attn_keys, value_weight, decoder, targets, send_rows, neighbours, live_slots, loss_multiplier):
    vm = pl.BlockSpec(memory_space=pltpu.VMEM)
    sm = pl.BlockSpec(memory_space=pltpu.SMEM)

    def buf(*shape, dtype=BF16):
        return pltpu.VMEM(shape, dtype)

    scratch = [
        buf(2, 4, 4, 4, 16, 512),
        buf(D, D),
        buf(M, W, D),
        buf(M, W, D),
        buf(M, D, R),
        buf(M, D, R),
        buf(2, M, D, W),
        buf(W, 2 * R, dtype=F32),
        buf(R, 2 * H),
        buf(2, M, H, D),
        buf(2, M, H, D),
        buf(D, 128),
        buf(128, D),
        buf(16, R, dtype=F32),
        buf(M, PAIRS, W, 2 * R, dtype=F32),
        buf(M, PAIRS, W, 2 * R),
        buf(M, W, D),
        buf(M, D, R),
        buf(M, 8, 16, R, dtype=F32),
        buf(MEMBERS, 16, R, dtype=F32),
        buf(MEMBERS, 16, R),
        buf(8, M, 16, R),
        buf(M, D, R),
        buf(2, M, W, 512),
        buf(M, W, D),
        buf(2, M, 2 * H, 512),
        buf(M, 2 * H, D),
        buf(4, 256, 512),
        buf(4, 256, 512),
        buf(3, 256, 512),
        buf(3, 256, 512),
        buf(4, 4, 16, 512, dtype=F32),
        buf(3, 4, 16, 512),
        buf(3, 4, 16, 512),
        buf(4, 16, 512, dtype=F32),
        buf(3, 16, 512),
        buf(3, 16, 512),
        buf(16, 512),
        buf(4, 16, 512),
        buf(2, 16, 512, dtype=F32),
        buf(6, 8, 128, dtype=F32),
        buf(6, 4, 8, 128, dtype=F32),
        pltpu.SemaphoreType.DMA((N_COPIES,)),
        pltpu.SemaphoreType.DMA((N_COPIES,)),
    ]
    loss, dl, dq, dk, dw = pl.pallas_call(
        kernel,
        out_shape=(
            jax.ShapeDtypeStruct((1, 1), F32),
            jax.ShapeDtypeStruct((M, R, D), BF16),
            jax.ShapeDtypeStruct((M, R, D), BF16),
            jax.ShapeDtypeStruct((M, R, D), BF16),
            jax.ShapeDtypeStruct((16, D), F32),
        ),
        in_specs=[vm] * 9 + [sm],
        out_specs=(sm, vm, vm, vm, vm),
        scratch_shapes=scratch,
        compiler_params=pltpu.CompilerParams(
            collective_id=0, has_side_effects=True, vmem_limit_bytes=56 * 1024 * 1024
        ),
    )(
        latents, queries, attn_keys, value_weight, decoder, targets, send_rows, neighbours,
        live_slots.reshape(1, R), loss_multiplier,
    )
    return loss.reshape(1), dl, dq, dk, dw


def solution(mesh):
    rows = P("ens", "space", None)
    in_specs = (
        rows, rows, rows, P("space", None), P(), P(None, "space"), P(None, "space"),
        P("space", None), P("space"), P(),
    )
    out_specs = (P(), rows, rows, rows, P("space", None))
    return jax.shard_map(body, mesh=mesh, in_specs=in_specs, out_specs=out_specs, check_vma=False)
```

```python
import jax
import jax.numpy as jnp
from jax import lax
from jax.experimental import pallas as pl
from jax.experimental.pallas import tpu as pltpu
from jax.sharding import PartitionSpec as P

MESH = pl.DeviceIdType.MESH
F32 = jnp.float32
BF16 = jnp.bfloat16
M, R, D, H, W = 2, 128, 1024, 32, 192
PAIRS = 8
CH = 13
MEMBERS = 16
CHANNELS = 100
SMOOTH = 0.1
NT = (((1,), (1,)), ((), ()))
TN = (((0,), (0,)), ((), ()))


def dot(a, b, dims=(((1,), (0,)), ((), ()))):
    return lax.dot_general(a, b, dims, preferred_element_type=F32)


def iota(shape, dim):
    return lax.broadcasted_iota(jnp.int32, shape, dim)


def kernel(
    L, Q, K, wsh, dec_h, tgt_h, srows_h, nbr_h, live_h, mult_h,
    o_loss, o_dl, o_dq, o_dk, o_dw,
    dec, tgt, srows, nbr, live, mult, qv,
    wg, wf, wl, kw, qt, lt, wlt, lk, oneh, snd_l, snd_k,
    decp, decpt, tgo, pf, pb, vv, outt, fs, fa, slf, terms, sl, sr, dot_t, dv, dk, rv, rk,
    e1s, e1r, s1, r1, a2, s2, r2, a3, s3, r3, s4, r4, fin, lsend, lrecv, gl, gq, gk, gw,
    ssem, rsem, lsem,
):
    e = lax.axis_index("ens")
    s = lax.axis_index("space")
    zh, c = e // 2, e % 2
    zl, y, x = s // 16, (s // 4) % 4, s % 4
    a = y * (1 - c) + x * c
    b = x * (1 - c) + y * c
    b_other = y * (1 - c) + x * c

    def at(e_, zl_, y_, x_):
        return (e_, zl_ * 16 + y_ * 4 + x_)

    sibling = (zh * 2 + 1 - c, s)

    def peer_a(k):
        return at(e, zl, (y + k * (1 - c)) % 4, (x + k * c) % 4)

    def peer_b(k):
        return at(e, zl, (y + k * c) % 4, (x + k * (1 - c)) % 4)

    def peer_zl(k):
        return at(e, (zl + k) % 4, y, x)

    def peer_zh(k):
        return (((zh + k) % 4) * 2 + c, s)

    def peer_ens(k):
        return ((e + k) % 8, s)

    right = (e, (s + 1) % 64)
    left = (e, (s + 63) % 64)

    barrier = pltpu.get_barrier_semaphore()
    partners = [peer_a(k) for k in (1, 2, 3)] + [peer_b(k) for k in (1, 2, 3)]
    partners += [peer_zl(k) for k in (1, 2, 3)] + [peer_ens(k) for k in range(1, 8)]
    partners += [right, left]
    for p in partners:
        pl.semaphore_signal(barrier, inc=1, device_id=p, device_id_type=MESH)

    sent = []
    count = [0]

    def send(src, dst, device):
        k = count[0]
        count[0] += 1
        copy = pltpu.make_async_remote_copy(
            src_ref=src, dst_ref=dst, send_sem=ssem.at[k], recv_sem=rsem.at[k],
            device_id=device, device_id_type=MESH,
        )
        copy.start()
        sent.append(copy)
        return copy

    fetched = []

    def fetch(src, dst):
        copy = pltpu.make_async_copy(src, dst, lsem.at[len(fetched)])
        fetched.append(copy)
        copy.start()
        return copy

    get_rows = fetch(srows_h, srows)
    get_k = fetch(K, kw.at[:, pl.ds(0, R)])
    get_l = fetch(L, wl.at[:, pl.ds(0, R)])
    own_half = pl.ds(pl.multiple_of(c * 512, 512), 512)
    get_w = fetch(wsh.at[:, own_half], wg.at[c, b, zl, a])
    get_q = fetch(Q, qv)
    get_small = [
        fetch(nbr_h, nbr), fetch(live_h, live), fetch(dec_h, dec), fetch(tgt_h, tgt), fetch(mult_h, mult)
    ]

    get_rows.wait()
    rows = iota((R, H), 0)
    to_right = (rows == srows[1:2, :]).astype(F32).astype(BF16)
    to_left = (rows == srows[0:1, :]).astype(F32).astype(BF16)
    oneh[:, 0:H] = to_right
    oneh[:, H:2 * H] = to_left
    get_k.wait()
    for m in range(M):
        snd_k[0, m] = dot(to_right, kw[m, 0:R], TN).astype(BF16)
        snd_k[1, m] = dot(to_left, kw[m, 0:R], TN).astype(BF16)
    get_l.wait()
    for m in range(M):
        snd_l[0, m] = dot(to_right, wl[m, 0:R], TN).astype(BF16)
        snd_l[1, m] = dot(to_left, wl[m, 0:R], TN).astype(BF16)
    get_w.wait()

    pl.semaphore_wait(barrier, len(partners))

    w1 = [send(wg.at[c, b, zl, a], wg.at[c, b, zl, a], peer_zl(k)) for k in (1, 2, 3)]
    hk = [
        send(snd_k.at[0], kw.at[:, pl.ds(R, H)], right),
        send(snd_k.at[1], kw.at[:, pl.ds(R + H, H)], left),
    ]

    def halo_latents():
        return [
            send(snd_l.at[0], wl.at[:, pl.ds(R, H)], right),
            send(snd_l.at[1], wl.at[:, pl.ds(R + H, H)], left),
        ]

    if HALO_AT == 0:
        hl = halo_latents()

    for copy in get_small:
        copy.wait()
    node_ids = nbr[...]
    row = iota((W, R), 0)
    wide_id = jnp.where(row < R, row + H, jnp.where(row < R + H, row - R, row))
    used = live[...]
    links = jnp.zeros((W, R), F32)
    for t in range(16):
        hit = jnp.where(used > t, node_ids[t:t + 1, :], -1) == wide_id
        links = links + jnp.where(hit, 1.0, 0.0)
    lk[:, 0:R] = links
    lk[:, R:2 * R] = links

    for k in range(3):
        w1[k].wait_recv()
    w2 = [send(wg.at[c, b, :, a], wg.at[c, b, :, a], peer_a(k)) for k in (1, 2, 3)]
    if HALO_AT == 2:
        hl = halo_latents()

    get_q.wait()
    for m in range(M):
        for d in range(8):
            qt[m, d * 128:(d + 1) * 128, :] = qv[m, :, d * 128:(d + 1) * 128].T
            lt[m, d * 128:(d + 1) * 128, :] = wl[m, 0:R, d * 128:(d + 1) * 128].T
    slot, chan = iota((128, CHANNELS), 0), iota((128, CHANNELS), 1)
    place = ((slot % 16 < CH) & (chan == (slot // 16) * CH + slot % 16)).astype(F32).astype(BF16)
    slot_t, chan_t = iota((CHANNELS, 128), 1), iota((CHANNELS, 128), 0)
    place_t = ((slot_t % 16 < CH) & (chan_t == (slot_t // 16) * CH + slot_t % 16)).astype(F32).astype(BF16)
    decp[...] = dot(dec[...], place_t, TN).astype(BF16)
    decpt[...] = dot(place, dec[...]).astype(BF16)
    slot16, chan16 = iota((16, CHANNELS), 0), iota((16, CHANNELS), 1)
    own_place = ((slot16 < CH) & (chan16 == e * CH + slot16)).astype(F32)
    tgo[...] = lax.dot_general(
        own_place, tgt[...], (((1,), (0,)), ((), ())),
        precision=lax.Precision.HIGHEST, preferred_element_type=F32,
    )

    for k in range(3):
        w2[k].wait_recv()
    w3 = [send(wg.at[c, b], wg.at[c, b], peer_b(k)) for k in (1, 2, 3)]
    wd = [send(wg.at[c, b], wg.at[c, b], sibling)]
    if HALO_AT == 3:
        hl = halo_latents()

    for k in range(2):
        hk[k].wait_recv()

    top = iota((128, R), 0) < 64

    def spread(block):
        zero = jnp.zeros_like(block)
        return jnp.concatenate([jnp.where(top, block, zero), jnp.where(top, zero, block)], axis=1)

    def folded(block):
        return jnp.where(top, block[:, 0:R], block[:, R:2 * R])

    def cols(p):
        return pl.ds(pl.multiple_of(p * 128, 128), 128)

    def weights_of(p, _):
        link = lk[...]
        for m in range(M):
            scores = dot(kw[m, :, cols(p)], spread(qt[m, cols(p), :])) * 0.125
            masked = jnp.where(link > 0, scores, -1e30)
            raised = link * jnp.exp(masked - jnp.max(masked, axis=0, keepdims=True))
            weight = raised * (1.0 / jnp.sum(raised, axis=0, keepdims=True))
            pf[m, p] = weight
            pb[m, p] = weight.astype(BF16)
        return 0

    lax.fori_loop(0, 4, weights_of, 0)
    for k in range(3):
        w3[k].wait_recv()
        bk = (b + 3 - k) % 4
        wd.append(send(wg.at[c, bk], wg.at[c, bk], sibling))
    lax.fori_loop(4, PAIRS, weights_of, 0)
    for k in range(2):
        hl[k].wait_recv()
    for k in range(4):
        wd[k].wait_recv()

    for z_ in range(4):
        for y_ in range(4):
            for x_ in range(4):
                d = z_ * 256 + y_ * 64 + x_ * 16
                wf[d:d + 16, 0:512] = wg[0, x_, z_, y_]
                wf[d:d + 16, 512:1024] = wg[1, y_, z_, x_]

    def mix(m):
        def step(p, _):
            mixed = folded(dot(vv[m, :, cols(p)], pb[m, p], TN))
            outt[m, cols(p), :] = (lt[m, cols(p), :].astype(F32) + mixed).astype(BF16)
            return 0
        return step

    def values_of(m):
        def step(q, _):
            block = pl.ds(pl.multiple_of(q * 256, 256), 256)
            vv[m, :, block] = dot(wl[m], wf[:, block]).astype(BF16)
            return 0
        return step

    fx = []
    for m in range(M):
        lax.fori_loop(0, 4, values_of(m), 0)
        lax.fori_loop(0, PAIRS, mix(m), 0)
        fs[m] = dot(decpt[...], outt[m]).reshape(8, 16, R)
        fa[2 * e + m] = fs[m, e]
        for k in range(1, 8):
            fx.append(send(fs.at[m, (e + k) % 8], fa.at[2 * e + m], peer_ens(k)))

    for m in range(M):
        for d in range(8):
            halo_t = wl[m, R:W, d * 128:(d + 1) * 128].T
            own_t = lt[m, d * 128:(d + 1) * 128, :]
            for i in range(8):
                g = d * 8 + i
                z_, y_, x_ = g // 16, (g // 4) % 4, g % 4
                r0 = (x_ * 16 + z_ * 4 + y_) * 16
                r1_ = (y_ * 16 + z_ * 4 + x_) * 16
                for h, r_ in ((0, r0), (1, r1_)):
                    wlt[h, m, r_:r_ + 16, 0:R] = own_t[i * 16:(i + 1) * 16]
                    wlt[h, m, r_:r_ + 16, R:W] = halo_t[i * 16:(i + 1) * 16]

    for copy in fx:
        copy.wait_recv()

    pair_norm = 1.0 / (MEMBERS * (MEMBERS - 1))

    def score(g, _):
        part = pl.ds(pl.multiple_of(g * 8, 8), 8)
        f = fa[:, part]
        shift = f - tgo[part][None]
        square = shift * shift + SMOOTH * SMOOTH
        inverse = lax.rsqrt(square)
        near = jnp.sum(square * inverse - SMOOTH, axis=0)
        pair_slope = jnp.zeros((MEMBERS, 8, R), F32)
        pair_total = jnp.zeros((8, R), F32)
        for k in range(1, 9):
            gap = f - jnp.concatenate([f[k:], f[:k]], axis=0)
            gap_square = gap * gap + SMOOTH * SMOOTH
            gap_inverse = lax.rsqrt(gap_square)
            radius = gap_square * gap_inverse - SMOOTH
            slope = gap * gap_inverse
            if k < 8:
                pair_total = pair_total + jnp.sum(radius, axis=0)
                back = jnp.concatenate([slope[MEMBERS - k:], slope[:MEMBERS - k]], axis=0)
                pair_slope = pair_slope + slope - back
            else:
                pair_total = pair_total + jnp.sum(radius[:8], axis=0)
                pair_slope = pair_slope + slope
        slf[:, part] = mult[0] * (shift * inverse * (1.0 / MEMBERS) - pair_slope * pair_norm)
        slot_id = iota((8, R), 0) + g * 8
        real = (slot_id < CH) & (slot_id + e * CH < CHANNELS)
        terms[g] = jnp.where(real, near * (1.0 / MEMBERS) - pair_total * pair_norm, 0.0)
        return 0

    lax.fori_loop(0, 2, score, 0)
    sl[...] = slf[...].astype(BF16)
    sx = [
        send(sl.at[pl.ds(2 * ((e + k) % 8), 2)], sr.at[e], peer_ens(k))
        for k in range(1, 8)
    ]
    sr[e] = sl[pl.ds(2 * e, 2)]
    lsend[0] = jnp.sum(terms[0] + terms[1], axis=0, keepdims=True)
    lrecv[0, zh] = lsend[0]
    l0 = [send(lsend.at[0], lrecv.at[0, zh], peer_zh(k)) for k in (1, 2, 3)]
    for copy in sx:
        copy.wait_recv()

    for m in range(M):
        dot_t[m] = dot(decp[...], sr[:, m].reshape(128, R)).astype(BF16)

    def value_grads(half, q):
        for i in range(2):
            p = half * 4 + q * 2 + i
            for m in range(M):
                dv[half, m, :, (q * 2 + i) * 128:(q * 2 + i + 1) * 128] = dot(
                    pb[m, p], spread(dot_t[m, cols(p), :]), NT
                ).astype(BF16)

    def weight_grad(half, q, block):
        block_rows = pl.ds(pl.multiple_of(block * 256, 256), 256)
        return dot(wlt[half, 0, block_rows, :], dv[half, 0, :, q * 256:(q + 1) * 256]) + dot(
            wlt[half, 1, block_rows, :], dv[half, 1, :, q * 256:(q + 1) * 256])

    def loss_step(stage, copies, mine, peers):
        for copy in copies:
            copy.wait_recv()
        got = lrecv[stage]
        if stage == 1:
            lsend[2] = got[0] + got[1]
        else:
            lsend[stage + 1] = (got[0] + got[1]) + (got[2] + got[3])
        lrecv[stage + 1, mine] = lsend[stage + 1]
        return [send(lsend.at[stage + 1], lrecv.at[stage + 1, mine], p) for p in peers]

    x1, x2, x3, x4, x5, x6 = ([None, None] for _ in range(6))
    for q in range(2):
        value_grads(1 - c, q)
        x1[q] = []
        for k in (1, 2, 3, 0):
            e1s[q, k] = weight_grad(1 - c, q, (b_other + k) % 4).astype(BF16)
            x1[q].append(send(e1s.at[q, k], e1r.at[q, k], sibling))
        value_grads(c, q)
        if q == 0:
            l1 = loss_step(0, l0, c, [sibling])
        else:
            hv = [
                send(dv.at[:, :, pl.ds(R + H, H)], rv.at[:, :, pl.ds(H, H)], right),
                send(dv.at[:, :, pl.ds(R, H)], rv.at[:, :, pl.ds(0, H)], left),
            ]
        x2[q] = []
        for i, k in enumerate((1, 2, 3, 0)):
            total = weight_grad(c, q, (b + k) % 4)
            x1[q][i].wait_recv()
            total = total + e1r[q, k].astype(F32)
            if k:
                s1[q, k - 1] = total.astype(BF16)
                x2[q].append(send(s1.at[q, k - 1], r1.at[q, k - 1], peer_b(k)))
            else:
                a2[q] = total.reshape(4, 4, 16, 256)

    def attention_grads(p, _):
        for m in range(M):
            grad_weight = dot(vv[m, :, cols(p)], spread(dot_t[m, cols(p), :])).astype(BF16).astype(F32)
            weight = pf[m, p]
            drift = jnp.sum(grad_weight * weight, axis=0, keepdims=True)
            grad_scores = (weight * (grad_weight - drift) * 0.125).astype(BF16)
            dk[m, :, cols(p)] = dot(grad_scores, spread(qt[m, cols(p), :]), NT).astype(BF16)
            grad_q = folded(dot(kw[m, :, cols(p)], grad_scores, TN))
            gq[m, :, cols(p)] = grad_q.astype(BF16).T
        return 0

    def second(q):
        for copy in x2[q]:
            copy.wait_recv()
        a2[q] = a2[q] + (
            r1[q, 0].astype(F32) + r1[q, 1].astype(F32) + r1[q, 2].astype(F32)
        ).reshape(4, 4, 16, 256)
        x3[q] = []
        for k in (1, 2, 3):
            s2[q, k - 1] = a2[q, :, (a + k) % 4].astype(BF16)
            x3[q].append(send(s2.at[q, k - 1], r2.at[q, k - 1], peer_a(k)))

    def third(q):
        for copy in x3[q]:
            copy.wait_recv()
        a3[q] = a2[q, :, a] + (r2[q, 0].astype(F32) + r2[q, 1].astype(F32) + r2[q, 2].astype(F32))
        x4[q] = []
        for k in (1, 2, 3):
            s3[q, k - 1] = a3[q, (zl + k) % 4].astype(BF16)
            x4[q].append(send(s3.at[q, k - 1], r3.at[q, k - 1], peer_zl(k)))

    def fourth(q):
        for copy in x4[q]:
            copy.wait_recv()
        s4[q] = (
            a3[q, zl] + (r3[q, 0].astype(F32) + r3[q, 1].astype(F32) + r3[q, 2].astype(F32))
        ).astype(BF16)
        r4[q, zh] = s4[q]
        x5[q] = [send(s4.at[q], r4.at[q, zh], peer_zh(k)) for k in (1, 2, 3)]

    def fifth(q):
        for copy in x5[q]:
            copy.wait_recv()
        fin[c, q] = (r4[q, 0].astype(F32) + r4[q, 1].astype(F32)) + (
            r4[q, 2].astype(F32) + r4[q, 3].astype(F32))
        x6[q] = send(fin.at[c, q], fin.at[c, q], sibling)

    def latent_grads(m):
        parts = [
            (dv[h, m, 0:R].astype(F32) + dot(oneh[...], rv[h, m])).astype(BF16) for h in range(2)
        ]
        out = dot(sr[:, m].reshape(128, R), decpt[...], TN).astype(BF16).astype(F32)
        out = out + dot(parts[0], wf[:, 0:512], NT) + dot(parts[1], wf[:, 512:1024], NT)
        gl[m] = out.astype(BF16)

    lax.fori_loop(0, 2, attention_grads, 0)
    l2 = loss_step(1, l1, b, [peer_b(k) for k in (1, 2, 3)])
    second(0)
    lax.fori_loop(2, 4, attention_grads, 0)
    second(1)
    lax.fori_loop(4, 6, attention_grads, 0)
    l3 = loss_step(2, l2, a, [peer_a(k) for k in (1, 2, 3)])
    third(0)
    lax.fori_loop(6, PAIRS, attention_grads, 0)
    third(1)
    hkb = [
        send(dk.at[:, pl.ds(R + H, H)], rk.at[:, pl.ds(H, H)], right),
        send(dk.at[:, pl.ds(R, H)], rk.at[:, pl.ds(0, H)], left),
    ]
    store = [fetch(gq, o_dq)]
    l4 = loss_step(3, l3, zl, [peer_zl(k) for k in (1, 2, 3)])
    for copy in hv:
        copy.wait_recv()
    fourth(0)
    latent_grads(0)
    fourth(1)
    latent_grads(1)
    store.append(fetch(gl, o_dl))
    l5 = loss_step(4, l4, c, [sibling])
    for copy in hkb:
        copy.wait_recv()
    for m in range(M):
        gk[m] = (dk[m, 0:R].astype(F32) + dot(oneh[...], rk[m])).astype(BF16)
    store.append(fetch(gk, o_dk))
    fifth(0)
    fifth(1)
    l5[0].wait_recv()
    o_loss[0, 0] = jnp.sum(lrecv[5, 0]) * (1.0 / (8192 * CHANNELS))
    for q in range(2):
        x6[q].wait_recv()
        for h in range(2):
            gw[:, h * 512 + q * 256:h * 512 + (q + 1) * 256] = fin[h, q]
    store.append(fetch(gw, o_dw))
    for copy in sent:
        copy.wait_send()
    for copy in store:
        copy.wait()


def hand_over(*refs):
    sources, results, held, sems = refs[:4], refs[4:8], refs[8:12], refs[12]
    arriving = [pltpu.make_async_copy(sources[i], held[i], sems.at[0, i]) for i in range(4)]
    leaving = [pltpu.make_async_copy(held[i], results[i], sems.at[1, i]) for i in range(4)]
    for copy in arriving:
        copy.start()
    for i in range(4):
        arriving[i].wait()
        leaving[i].start()
    for copy in leaving:
        copy.wait()


HALO_AT = 2
N_COPIES = 112


def body(latents, queries, attn_keys, value_weight, decoder, targets, send_rows, neighbours, live_slots, loss_multiplier):
    hbm = pl.BlockSpec(memory_space=pl.ANY)
    sm = pl.BlockSpec(memory_space=pltpu.SMEM)

    def buf(*shape, dtype=BF16):
        return pltpu.VMEM(shape, dtype)

    scratch = [
        buf(CHANNELS, D),
        buf(CHANNELS, R, dtype=F32),
        buf(2, H, dtype=jnp.int32),
        buf(16, R, dtype=jnp.int32),
        buf(1, R, dtype=jnp.int32),
        pltpu.SMEM((1,), F32),
        buf(M, R, D),
        buf(2, 4, 4, 4, 16, 512),
        buf(D, D),
        buf(M, W, D),
        buf(M, W, D),
        buf(M, D, R),
        buf(M, D, R),
        buf(2, M, D, W),
        buf(W, 2 * R, dtype=F32),
        buf(R, 2 * H),
        buf(2, M, H, D),
        buf(2, M, H, D),
        buf(D, 128),
        buf(128, D),
        buf(16, R, dtype=F32),
        buf(M, PAIRS, W, 2 * R, dtype=F32),
        buf(M, PAIRS, W, 2 * R),
        buf(M, W, D),
        buf(M, D, R),
        buf(M, 8, 16, R, dtype=F32),
        buf(MEMBERS, 16, R, dtype=F32),
        buf(MEMBERS, 16, R, dtype=F32),
        buf(2, 8, R, dtype=F32),
        buf(MEMBERS, 16, R),
        buf(8, M, 16, R),
        buf(M, D, R),
        buf(2, M, W, 512),
        buf(M, W, D),
        buf(2, M, 2 * H, 512),
        buf(M, 2 * H, D),
        buf(2, 4, 256, 256),
        buf(2, 4, 256, 256),
        buf(2, 3, 256, 256),
        buf(2, 3, 256, 256),
        buf(2, 4, 4, 16, 256, dtype=F32),
        buf(2, 3, 4, 16, 256),
        buf(2, 3, 4, 16, 256),
        buf(2, 4, 16, 256, dtype=F32),
        buf(2, 3, 16, 256),
        buf(2, 3, 16, 256),
        buf(2, 16, 256),
        buf(2, 4, 16, 256),
        buf(2, 2, 16, 256, dtype=F32),
        buf(6, 1, 128, dtype=F32),
        buf(6, 4, 1, 128, dtype=F32),
        buf(M, R, D),
        buf(M, R, D),
        buf(M, R, D),
        buf(16, D, dtype=F32),
        pltpu.SemaphoreType.DMA((N_COPIES,)),
        pltpu.SemaphoreType.DMA((N_COPIES,)),
        pltpu.SemaphoreType.DMA((16,)),
    ]
    loss, dl, dq, dk, dw = pl.pallas_call(
        kernel,
        out_shape=(
            jax.ShapeDtypeStruct((1, 1), F32),
            jax.ShapeDtypeStruct((M, R, D), BF16),
            jax.ShapeDtypeStruct((M, R, D), BF16),
            jax.ShapeDtypeStruct((M, R, D), BF16),
            jax.ShapeDtypeStruct((16, D), F32),
        ),
        in_specs=[hbm] * 10,
        out_specs=(sm, hbm, hbm, hbm, hbm),
        scratch_shapes=scratch,
        compiler_params=pltpu.CompilerParams(
            collective_id=0, has_side_effects=True, vmem_limit_bytes=56 * 1024 * 1024
        ),
    )(
        latents, queries, attn_keys, value_weight, decoder.T, targets, send_rows, neighbours.T,
        live_slots.reshape(1, R), loss_multiplier,
    )
    results = (dl, dq, dk, dw)
    dl, dq, dk, dw = pl.pallas_call(
        hand_over,
        out_shape=tuple(jax.ShapeDtypeStruct(r.shape, r.dtype) for r in results),
        in_specs=[hbm] * 4,
        out_specs=(hbm,) * 4,
        scratch_shapes=[pltpu.VMEM(r.shape, r.dtype) for r in results] + [pltpu.SemaphoreType.DMA((2, 4))],
    )(*results)
    return loss.reshape(1), dl, dq, dk, dw


def solution(mesh):
    rows = P("ens", "space", None)
    in_specs = (
        rows, rows, rows, P("space", None), P(), P(None, "space"), P(None, "space"),
        P("space", None), P("space"), P(),
    )
    out_specs = (P(), rows, rows, rows, P("space", None))
    return jax.shard_map(body, mesh=mesh, in_specs=in_specs, out_specs=out_specs, check_vma=False)
```

```python
import jax
import jax.numpy as jnp
from jax import lax
from jax.experimental import pallas as pl
from jax.experimental.pallas import tpu as pltpu
from jax.sharding import PartitionSpec as P

MESH = pl.DeviceIdType.MESH
F32 = jnp.float32
BF16 = jnp.bfloat16
M, R, D, H, W = 2, 128, 1024, 32, 192
PAIRS = 8
CH = 13
MEMBERS = 16
CHANNELS = 100
SMOOTH = 0.1
NT = (((1,), (1,)), ((), ()))
TN = (((0,), (0,)), ((), ()))


def dot(a, b, dims=(((1,), (0,)), ((), ()))):
    return lax.dot_general(a, b, dims, preferred_element_type=F32)


def iota(shape, dim):
    return lax.broadcasted_iota(jnp.int32, shape, dim)


def kernel(
    L, Q, K, wsh, dec_h, tgt_h, srows_h, nbr_h, live_h, mult_h,
    o_loss, o_dl, o_dq, o_dk, o_dw,
    dec, tgt, srows, nbr, live, mult, qv,
    wg, wf, wl, kw, qt, lt, wlt, lk, oneh, snd_l, snd_k,
    decp, decpt, tgo, pf, pb, vv, outt, fs, fa, slf, terms, sl, sr, dot_t, dv, dk, rv, rk,
    e1s, e1r, s1, r1, a2, s2, r2, a3, s3, r3, s4, r4, fin, lsend, lrecv, gl, gq, gk, gw,
    ssem, rsem, lsem,
):
    e = lax.axis_index("ens")
    s = lax.axis_index("space")
    zh, c = e // 2, e % 2
    zl, y, x = s // 16, (s // 4) % 4, s % 4
    a = y * (1 - c) + x * c
    b = x * (1 - c) + y * c
    b_other = y * (1 - c) + x * c

    def at(e_, zl_, y_, x_):
        return (e_, zl_ * 16 + y_ * 4 + x_)

    sibling = (zh * 2 + 1 - c, s)

    def peer_a(k):
        return at(e, zl, (y + k * (1 - c)) % 4, (x + k * c) % 4)

    def peer_b(k):
        return at(e, zl, (y + k * c) % 4, (x + k * (1 - c)) % 4)

    def peer_zl(k):
        return at(e, (zl + k) % 4, y, x)

    def peer_zh(k):
        return (((zh + k) % 4) * 2 + c, s)

    def peer_ens(k):
        return ((e + k) % 8, s)

    right = (e, (s + 1) % 64)
    left = (e, (s + 63) % 64)

    barrier = pltpu.get_barrier_semaphore()
    partners = [peer_a(k) for k in (1, 2, 3)] + [peer_b(k) for k in (1, 2, 3)]
    partners += [peer_zl(k) for k in (1, 2, 3)] + [peer_ens(k) for k in range(1, 8)]
    partners += [right, left]
    for p in partners:
        pl.semaphore_signal(barrier, inc=1, device_id=p, device_id_type=MESH)

    sent = []
    count = [0]

    def send(src, dst, device):
        k = count[0]
        count[0] += 1
        copy = pltpu.make_async_remote_copy(
            src_ref=src, dst_ref=dst, send_sem=ssem.at[k], recv_sem=rsem.at[k],
            device_id=device, device_id_type=MESH,
        )
        copy.start()
        sent.append(copy)
        return copy

    fetched = []

    def fetch(src, dst):
        copy = pltpu.make_async_copy(src, dst, lsem.at[len(fetched)])
        fetched.append(copy)
        copy.start()
        return copy

    get_rows = fetch(srows_h, srows)
    get_k = fetch(K, kw.at[:, pl.ds(0, R)])
    get_l = fetch(L, wl.at[:, pl.ds(0, R)])
    own_half = pl.ds(pl.multiple_of(c * 512, 512), 512)
    get_w = fetch(wsh.at[:, own_half], wg.at[c, b, zl, a])
    get_q = fetch(Q, qv)
    get_small = [
        fetch(nbr_h, nbr), fetch(live_h, live), fetch(dec_h, dec), fetch(tgt_h, tgt), fetch(mult_h, mult)
    ]

    get_rows.wait()
    rows = iota((R, H), 0)
    to_right = (rows == srows[1:2, :]).astype(F32).astype(BF16)
    to_left = (rows == srows[0:1, :]).astype(F32).astype(BF16)
    oneh[:, 0:H] = to_right
    oneh[:, H:2 * H] = to_left
    get_k.wait()
    for m in range(M):
        snd_k[0, m] = dot(to_right, kw[m, 0:R], TN).astype(BF16)
        snd_k[1, m] = dot(to_left, kw[m, 0:R], TN).astype(BF16)
    get_l.wait()
    for m in range(M):
        snd_l[0, m] = dot(to_right, wl[m, 0:R], TN).astype(BF16)
        snd_l[1, m] = dot(to_left, wl[m, 0:R], TN).astype(BF16)
    get_w.wait()

    pl.semaphore_wait(barrier, len(partners))

    w1 = [send(wg.at[c, b, zl, a], wg.at[c, b, zl, a], peer_zl(k)) for k in (1, 2, 3)]
    def halo_keys():
        return [
            send(snd_k.at[0], kw.at[:, pl.ds(R, H)], right),
            send(snd_k.at[1], kw.at[:, pl.ds(R + H, H)], left),
        ]

    hk = halo_keys()

    def halo_latents():
        return [
            send(snd_l.at[0], wl.at[:, pl.ds(R, H)], right),
            send(snd_l.at[1], wl.at[:, pl.ds(R + H, H)], left),
        ]

    for copy in get_small:
        copy.wait()
    node_ids = nbr[...]
    row = iota((W, R), 0)
    wide_id = jnp.where(row < R, row + H, jnp.where(row < R + H, row - R, row))
    used = live[...]
    links = jnp.zeros((W, R), F32)
    for t in range(16):
        hit = jnp.where(used > t, node_ids[t:t + 1, :], -1) == wide_id
        links = links + jnp.where(hit, 1.0, 0.0)
    lk[:, 0:R] = links
    lk[:, R:2 * R] = links

    for k in range(3):
        w1[k].wait_recv()
    w2 = [send(wg.at[c, b, :, a], wg.at[c, b, :, a], peer_a(k)) for k in (1, 2, 3)]
    hl = halo_latents()

    get_q.wait()
    for m in range(M):
        for d in range(8):
            qt[m, d * 128:(d + 1) * 128, :] = qv[m, :, d * 128:(d + 1) * 128].T
            lt[m, d * 128:(d + 1) * 128, :] = wl[m, 0:R, d * 128:(d + 1) * 128].T
    slot, chan = iota((128, CHANNELS), 0), iota((128, CHANNELS), 1)
    place = ((slot % 16 < CH) & (chan == (slot // 16) * CH + slot % 16)).astype(F32).astype(BF16)
    slot_t, chan_t = iota((CHANNELS, 128), 1), iota((CHANNELS, 128), 0)
    place_t = ((slot_t % 16 < CH) & (chan_t == (slot_t // 16) * CH + slot_t % 16)).astype(F32).astype(BF16)
    decp[...] = dot(dec[...], place_t, TN).astype(BF16)
    decpt[...] = dot(place, dec[...]).astype(BF16)
    slot16, chan16 = iota((16, CHANNELS), 0), iota((16, CHANNELS), 1)
    own_place = ((slot16 < CH) & (chan16 == e * CH + slot16)).astype(F32)
    tgo[...] = lax.dot_general(
        own_place, tgt[...], (((1,), (0,)), ((), ())),
        precision=lax.Precision.HIGHEST, preferred_element_type=F32,
    )

    for k in range(3):
        w2[k].wait_recv()
    w3 = [send(wg.at[c, b], wg.at[c, b], peer_b(k)) for k in (1, 2, 3)]
    wd = [send(wg.at[c, b], wg.at[c, b], sibling)]

    for k in range(2):
        hk[k].wait_recv()

    top = iota((128, R), 0) < 64

    def spread(block):
        zero = jnp.zeros_like(block)
        return jnp.concatenate([jnp.where(top, block, zero), jnp.where(top, zero, block)], axis=1)

    def folded(block):
        return jnp.where(top, block[:, 0:R], block[:, R:2 * R])

    def cols(p):
        return pl.ds(pl.multiple_of(p * 128, 128), 128)

    def weights_of(p, _):
        link = lk[...]
        for m in range(M):
            scores = dot(kw[m, :, cols(p)], spread(qt[m, cols(p), :])) * 0.125
            masked = jnp.where(link > 0, scores, -1e30)
            raised = link * jnp.exp(masked - jnp.max(masked, axis=0, keepdims=True))
            weight = raised * (1.0 / jnp.sum(raised, axis=0, keepdims=True))
            pf[m, p] = weight
            pb[m, p] = weight.astype(BF16)
        return 0

    lax.fori_loop(0, 4, weights_of, 0, unroll=2)
    for k in range(3):
        w3[k].wait_recv()
        bk = (b + 3 - k) % 4
        wd.append(send(wg.at[c, bk], wg.at[c, bk], sibling))
    lax.fori_loop(4, PAIRS, weights_of, 0, unroll=2)
    for k in range(2):
        hl[k].wait_recv()
    for k in range(4):
        wd[k].wait_recv()

    for z_ in range(4):
        for y_ in range(4):
            for x_ in range(4):
                d = z_ * 256 + y_ * 64 + x_ * 16
                wf[d:d + 16, 0:512] = wg[0, x_, z_, y_]
                wf[d:d + 16, 512:1024] = wg[1, y_, z_, x_]

    def mix(m):
        def step(p, _):
            mixed = folded(dot(vv[m, :, cols(p)], pb[m, p], TN))
            outt[m, cols(p), :] = (lt[m, cols(p), :].astype(F32) + mixed).astype(BF16)
            return 0
        return step

    def values_of(q, _):
        block = pl.ds(pl.multiple_of(q * 256, 256), 256)
        both = dot(wl[...].reshape(M * W, D), wf[:, block]).astype(BF16)
        for m in range(M):
            vv[m, :, block] = both[m * W:(m + 1) * W]
        return 0

    lax.fori_loop(0, 4, values_of, 0)
    fx = []
    for m in range(M):
        lax.fori_loop(0, PAIRS, mix(m), 0, unroll=4)
        fs[m] = dot(decpt[...], outt[m]).reshape(8, 16, R)
        fa[2 * e + m] = fs[m, e]
        for k in range(1, 8):
            fx.append(send(fs.at[m, (e + k) % 8], fa.at[2 * e + m], peer_ens(k)))

    for m in range(M):
        for d in range(8):
            halo_t = wl[m, R:W, d * 128:(d + 1) * 128].T
            own_t = lt[m, d * 128:(d + 1) * 128, :]
            for i in range(8):
                g = d * 8 + i
                z_, y_, x_ = g // 16, (g // 4) % 4, g % 4
                r0 = (x_ * 16 + z_ * 4 + y_) * 16
                r1_ = (y_ * 16 + z_ * 4 + x_) * 16
                for h, r_ in ((0, r0), (1, r1_)):
                    wlt[h, m, r_:r_ + 16, 0:R] = own_t[i * 16:(i + 1) * 16]
                    wlt[h, m, r_:r_ + 16, R:W] = halo_t[i * 16:(i + 1) * 16]

    for copy in fx:
        copy.wait_recv()

    pair_norm = 1.0 / (MEMBERS * (MEMBERS - 1))

    def score(g, _):
        part = pl.ds(pl.multiple_of(g * 8, 8), 8)
        f = fa[:, part]
        shift = f - tgo[part][None]
        square = shift * shift + SMOOTH * SMOOTH
        inverse = lax.rsqrt(square)
        near = jnp.sum(square * inverse - SMOOTH, axis=0)
        pair_slope = jnp.zeros((MEMBERS, 8, R), F32)
        pair_total = jnp.zeros((8, R), F32)
        for k in range(1, 9):
            gap = f - jnp.concatenate([f[k:], f[:k]], axis=0)
            gap_square = gap * gap + SMOOTH * SMOOTH
            gap_inverse = lax.rsqrt(gap_square)
            radius = gap_square * gap_inverse - SMOOTH
            slope = gap * gap_inverse
            if k < 8:
                pair_total = pair_total + jnp.sum(radius, axis=0)
                back = jnp.concatenate([slope[MEMBERS - k:], slope[:MEMBERS - k]], axis=0)
                pair_slope = pair_slope + slope - back
            else:
                pair_total = pair_total + jnp.sum(radius[:8], axis=0)
                pair_slope = pair_slope + slope
        slf[:, part] = mult[0] * (shift * inverse * (1.0 / MEMBERS) - pair_slope * pair_norm)
        slot_id = iota((8, R), 0) + g * 8
        real = (slot_id < CH) & (slot_id + e * CH < CHANNELS)
        terms[g] = jnp.where(real, near * (1.0 / MEMBERS) - pair_total * pair_norm, 0.0)
        return 0

    lax.fori_loop(0, 2, score, 0)
    sl[...] = slf[...].astype(BF16)
    sx = [
        send(sl.at[pl.ds(2 * ((e + k) % 8), 2)], sr.at[e], peer_ens(k))
        for k in range(1, 8)
    ]
    sr[e] = sl[pl.ds(2 * e, 2)]
    lsend[0] = jnp.sum(terms[0] + terms[1], axis=0, keepdims=True)
    lrecv[0, zh] = lsend[0]
    l0 = [send(lsend.at[0], lrecv.at[0, zh], peer_zh(k)) for k in (1, 2, 3)]
    for copy in sx:
        copy.wait_recv()

    for m in range(M):
        dot_t[m] = dot(decp[...], sr[:, m].reshape(128, R)).astype(BF16)

    def value_grads(half, q):
        for i in range(2):
            p = half * 4 + q * 2 + i
            for m in range(M):
                dv[half, m, :, (q * 2 + i) * 128:(q * 2 + i + 1) * 128] = dot(
                    pb[m, p], spread(dot_t[m, cols(p), :]), NT
                ).astype(BF16)

    def weight_grad(half, q, block):
        block_rows = pl.ds(pl.multiple_of(block * 256, 256), 256)
        return dot(wlt[half, 0, block_rows, :], dv[half, 0, :, q * 256:(q + 1) * 256]) + dot(
            wlt[half, 1, block_rows, :], dv[half, 1, :, q * 256:(q + 1) * 256])

    def loss_step(stage, copies, mine, peers):
        for copy in copies:
            copy.wait_recv()
        got = lrecv[stage]
        if stage == 1:
            lsend[2] = got[0] + got[1]
        else:
            lsend[stage + 1] = (got[0] + got[1]) + (got[2] + got[3])
        lrecv[stage + 1, mine] = lsend[stage + 1]
        return [send(lsend.at[stage + 1], lrecv.at[stage + 1, mine], p) for p in peers]

    x1, x2, x3, x4, x5, x6 = ([None, None] for _ in range(6))
    for q in range(2):
        value_grads(1 - c, q)
        x1[q] = []
        for k in (1, 2, 3, 0):
            e1s[q, k] = weight_grad(1 - c, q, (b_other + k) % 4).astype(BF16)
            x1[q].append(send(e1s.at[q, k], e1r.at[q, k], sibling))
        value_grads(c, q)
        x2[q] = []
        for i, k in enumerate((1, 2, 3, 0)):
            total = weight_grad(c, q, (b + k) % 4)
            x1[q][i].wait_recv()
            total = total + e1r[q, k].astype(F32)
            if k:
                s1[q, k - 1] = total.astype(BF16)
                x2[q].append(send(s1.at[q, k - 1], r1.at[q, k - 1], peer_b(k)))
            else:
                a2[q] = total.reshape(4, 4, 16, 256)

    hv = [
        send(dv.at[:, :, pl.ds(R + H, H)], rv.at[:, :, pl.ds(H, H)], right),
        send(dv.at[:, :, pl.ds(R, H)], rv.at[:, :, pl.ds(0, H)], left),
    ]
    l1 = loss_step(0, l0, c, [sibling])

    def attention_grads(p, _):
        for m in range(M):
            grad_weight = dot(vv[m, :, cols(p)], spread(dot_t[m, cols(p), :])).astype(BF16).astype(F32)
            weight = pf[m, p]
            drift = jnp.sum(grad_weight * weight, axis=0, keepdims=True)
            grad_scores = (weight * (grad_weight - drift) * 0.125).astype(BF16)
            dk[m, :, cols(p)] = dot(grad_scores, spread(qt[m, cols(p), :]), NT).astype(BF16)
            grad_q = folded(dot(kw[m, :, cols(p)], grad_scores, TN))
            gq[m, :, cols(p)] = grad_q.astype(BF16).T
        return 0

    def second(q):
        for copy in x2[q]:
            copy.wait_recv()
        a2[q] = a2[q] + (
            r1[q, 0].astype(F32) + r1[q, 1].astype(F32) + r1[q, 2].astype(F32)
        ).reshape(4, 4, 16, 256)
        x3[q] = []
        for k in (1, 2, 3):
            s2[q, k - 1] = a2[q, :, (a + k) % 4].astype(BF16)
            x3[q].append(send(s2.at[q, k - 1], r2.at[q, k - 1], peer_a(k)))

    def third(q):
        for copy in x3[q]:
            copy.wait_recv()
        a3[q] = a2[q, :, a] + (r2[q, 0].astype(F32) + r2[q, 1].astype(F32) + r2[q, 2].astype(F32))
        x4[q] = []
        for k in (1, 2, 3):
            s3[q, k - 1] = a3[q, (zl + k) % 4].astype(BF16)
            x4[q].append(send(s3.at[q, k - 1], r3.at[q, k - 1], peer_zl(k)))

    def fourth(q):
        for copy in x4[q]:
            copy.wait_recv()
        s4[q] = (
            a3[q, zl] + (r3[q, 0].astype(F32) + r3[q, 1].astype(F32) + r3[q, 2].astype(F32))
        ).astype(BF16)
        r4[q, zh] = s4[q]
        x5[q] = [send(s4.at[q], r4.at[q, zh], peer_zh(k)) for k in (1, 2, 3)]

    def fifth(q):
        for copy in x5[q]:
            copy.wait_recv()
        fin[c, q] = (r4[q, 0].astype(F32) + r4[q, 1].astype(F32)) + (
            r4[q, 2].astype(F32) + r4[q, 3].astype(F32))
        x6[q] = send(fin.at[c, q], fin.at[c, q], sibling)

    def latent_grads(m):
        parts = [
            (dv[h, m, 0:R].astype(F32) + dot(oneh[...], rv[h, m])).astype(BF16) for h in range(2)
        ]
        out = dot(sr[:, m].reshape(128, R), decpt[...], TN).astype(BF16).astype(F32)
        out = out + dot(parts[0], wf[:, 0:512], NT) + dot(parts[1], wf[:, 512:1024], NT)
        gl[m] = out.astype(BF16)

    lax.fori_loop(0, 2, attention_grads, 0, unroll=2)
    l2 = loss_step(1, l1, b, [peer_b(k) for k in (1, 2, 3)])
    second(0)
    lax.fori_loop(2, 4, attention_grads, 0, unroll=2)
    second(1)
    lax.fori_loop(4, 6, attention_grads, 0, unroll=2)
    l3 = loss_step(2, l2, a, [peer_a(k) for k in (1, 2, 3)])
    third(0)
    lax.fori_loop(6, PAIRS, attention_grads, 0, unroll=2)
    third(1)
    hkb = [
        send(dk.at[:, pl.ds(R + H, H)], rk.at[:, pl.ds(H, H)], right),
        send(dk.at[:, pl.ds(R, H)], rk.at[:, pl.ds(0, H)], left),
    ]
    store = [fetch(gq, o_dq)]
    l4 = loss_step(3, l3, zl, [peer_zl(k) for k in (1, 2, 3)])
    fourth(0)
    fourth(1)
    for copy in hv:
        copy.wait_recv()
    latent_grads(0)
    latent_grads(1)
    store.append(fetch(gl, o_dl))
    l5 = loss_step(4, l4, c, [sibling])
    for copy in hkb:
        copy.wait_recv()
    for m in range(M):
        gk[m] = (dk[m, 0:R].astype(F32) + dot(oneh[...], rk[m])).astype(BF16)
    store.append(fetch(gk, o_dk))
    fifth(0)
    fifth(1)
    l5[0].wait_recv()
    o_loss[0, 0] = jnp.sum(lrecv[5, 0]) * (1.0 / (8192 * CHANNELS))
    for q in range(2):
        x6[q].wait_recv()
        for h in range(2):
            gw[:, h * 512 + q * 256:h * 512 + (q + 1) * 256] = fin[h, q]
    store.append(fetch(gw, o_dw))
    for copy in sent:
        copy.wait_send()
    for copy in store:
        copy.wait()


def hand_over(*refs):
    sources, results, held, sems = refs[:4], refs[4:8], refs[8:12], refs[12]
    arriving = [pltpu.make_async_copy(sources[i], held[i], sems.at[0, i]) for i in range(4)]
    leaving = [pltpu.make_async_copy(held[i], results[i], sems.at[1, i]) for i in range(4)]
    for copy in arriving:
        copy.start()
    for i in range(4):
        arriving[i].wait()
        leaving[i].start()
    for copy in leaving:
        copy.wait()


N_COPIES = 112


def body(latents, queries, attn_keys, value_weight, decoder, targets, send_rows, neighbours, live_slots, loss_multiplier):
    hbm = pl.BlockSpec(memory_space=pl.ANY)
    sm = pl.BlockSpec(memory_space=pltpu.SMEM)

    def buf(*shape, dtype=BF16):
        return pltpu.VMEM(shape, dtype)

    scratch = [
        buf(CHANNELS, D),
        buf(CHANNELS, R, dtype=F32),
        buf(2, H, dtype=jnp.int32),
        buf(16, R, dtype=jnp.int32),
        buf(1, R, dtype=jnp.int32),
        pltpu.SMEM((1,), F32),
        buf(M, R, D),
        buf(2, 4, 4, 4, 16, 512),
        buf(D, D),
        buf(M, W, D),
        buf(M, W, D),
        buf(M, D, R),
        buf(M, D, R),
        buf(2, M, D, W),
        buf(W, 2 * R, dtype=F32),
        buf(R, 2 * H),
        buf(2, M, H, D),
        buf(2, M, H, D),
        buf(D, 128),
        buf(128, D),
        buf(16, R, dtype=F32),
        buf(M, PAIRS, W, 2 * R, dtype=F32),
        buf(M, PAIRS, W, 2 * R),
        buf(M, W, D),
        buf(M, D, R),
        buf(M, 8, 16, R, dtype=F32),
        buf(MEMBERS, 16, R, dtype=F32),
        buf(MEMBERS, 16, R, dtype=F32),
        buf(2, 8, R, dtype=F32),
        buf(MEMBERS, 16, R),
        buf(8, M, 16, R),
        buf(M, D, R),
        buf(2, M, W, 512),
        buf(M, W, D),
        buf(2, M, 2 * H, 512),
        buf(M, 2 * H, D),
        buf(2, 4, 256, 256),
        buf(2, 4, 256, 256),
        buf(2, 3, 256, 256),
        buf(2, 3, 256, 256),
        buf(2, 4, 4, 16, 256, dtype=F32),
        buf(2, 3, 4, 16, 256),
        buf(2, 3, 4, 16, 256),
        buf(2, 4, 16, 256, dtype=F32),
        buf(2, 3, 16, 256),
        buf(2, 3, 16, 256),
        buf(2, 16, 256),
        buf(2, 4, 16, 256),
        buf(2, 2, 16, 256, dtype=F32),
        buf(6, 1, 128, dtype=F32),
        buf(6, 4, 1, 128, dtype=F32),
        buf(M, R, D),
        buf(M, R, D),
        buf(M, R, D),
        buf(16, D, dtype=F32),
        pltpu.SemaphoreType.DMA((N_COPIES,)),
        pltpu.SemaphoreType.DMA((N_COPIES,)),
        pltpu.SemaphoreType.DMA((16,)),
    ]
    loss, dl, dq, dk, dw = pl.pallas_call(
        kernel,
        out_shape=(
            jax.ShapeDtypeStruct((1, 1), F32),
            jax.ShapeDtypeStruct((M, R, D), BF16),
            jax.ShapeDtypeStruct((M, R, D), BF16),
            jax.ShapeDtypeStruct((M, R, D), BF16),
            jax.ShapeDtypeStruct((16, D), F32),
        ),
        in_specs=[hbm] * 10,
        out_specs=(sm, hbm, hbm, hbm, hbm),
        scratch_shapes=scratch,
        compiler_params=pltpu.CompilerParams(
            collective_id=0, has_side_effects=True, vmem_limit_bytes=56 * 1024 * 1024
        ),
    )(
        latents, queries, attn_keys, value_weight, decoder.T, targets, send_rows, neighbours.T,
        live_slots.reshape(1, R), loss_multiplier,
    )
    results = (dl, dq, dk, dw)
    dl, dq, dk, dw = pl.pallas_call(
        hand_over,
        out_shape=tuple(jax.ShapeDtypeStruct(r.shape, r.dtype) for r in results),
        in_specs=[hbm] * 4,
        out_specs=(hbm,) * 4,
        scratch_shapes=[pltpu.VMEM(r.shape, r.dtype) for r in results] + [pltpu.SemaphoreType.DMA((2, 4))],
    )(*results)
    return loss.reshape(1), dl, dq, dk, dw


def solution(mesh):
    rows = P("ens", "space", None)
    in_specs = (
        rows, rows, rows, P("space", None), P(), P(None, "space"), P(None, "space"),
        P("space", None), P("space"), P(),
    )
    out_specs = (P(), rows, rows, rows, P("space", None))
    return jax.shard_map(body, mesh=mesh, in_specs=in_specs, out_specs=out_specs, check_vma=False)
```

```python
import jax
import jax.numpy as jnp
from jax import lax
from jax.experimental import pallas as pl
from jax.experimental.pallas import tpu as pltpu
from jax.sharding import PartitionSpec as P

MESH = pl.DeviceIdType.MESH
F32 = jnp.float32
BF16 = jnp.bfloat16
M, R, D, H, W = 2, 128, 1024, 32, 192
PAIRS = 8
CH = 13
MEMBERS = 16
CHANNELS = 100
SMOOTH = 0.1
NT = (((1,), (1,)), ((), ()))
TN = (((0,), (0,)), ((), ()))


def dot(a, b, dims=(((1,), (0,)), ((), ()))):
    return lax.dot_general(a, b, dims, preferred_element_type=F32)


def iota(shape, dim):
    return lax.broadcasted_iota(jnp.int32, shape, dim)


def kernel(
    L, Q, K, wsh, dec_h, tgt_h, srows_h, nbr_h, live_h, mult_h,
    o_loss, o_dl, o_dq, o_dk, o_dw,
    dec, tgt, srows, nbr, live, mult, qv,
    wg, wf, wl, kw, qt, lt, wlt, lk, oneh, snd_l, snd_k,
    decp, decpt, tgo, pf, pb, vv, outt, fs, fa, slf, terms, sl, sr, dot_t, dv, dk, rv, rk,
    e1s, e1r, s1, r1, a2, s2, r2, a3, s3, r3, s4, r4, fin, lsend, lrecv, gl, gq, gk, gw,
    ssem, rsem, lsem,
):
    e = lax.axis_index("ens")
    s = lax.axis_index("space")
    zh, c = e // 2, e % 2
    zl, y, x = s // 16, (s // 4) % 4, s % 4
    a = y * (1 - c) + x * c
    b = x * (1 - c) + y * c
    b_other = y * (1 - c) + x * c

    def at(e_, zl_, y_, x_):
        return (e_, zl_ * 16 + y_ * 4 + x_)

    sibling = (zh * 2 + 1 - c, s)

    def peer_a(k):
        return at(e, zl, (y + k * (1 - c)) % 4, (x + k * c) % 4)

    def peer_b(k):
        return at(e, zl, (y + k * c) % 4, (x + k * (1 - c)) % 4)

    def peer_zl(k):
        return at(e, (zl + k) % 4, y, x)

    def peer_zh(k):
        return (((zh + k) % 4) * 2 + c, s)

    def peer_ens(k):
        return ((e + k) % 8, s)

    right = (e, (s + 1) % 64)
    left = (e, (s + 63) % 64)

    barrier = pltpu.get_barrier_semaphore()
    partners = [peer_a(k) for k in (1, 2, 3)] + [peer_b(k) for k in (1, 2, 3)]
    partners += [peer_zl(k) for k in (1, 2, 3)] + [peer_ens(k) for k in range(1, 8)]
    partners += [right, left]
    for p in partners:
        pl.semaphore_signal(barrier, inc=1, device_id=p, device_id_type=MESH)

    sent = []
    count = [0]

    def send(src, dst, device):
        k = count[0]
        count[0] += 1
        copy = pltpu.make_async_remote_copy(
            src_ref=src, dst_ref=dst, send_sem=ssem.at[k], recv_sem=rsem.at[k],
            device_id=device, device_id_type=MESH,
        )
        copy.start()
        sent.append(copy)
        return copy

    fetched = []

    def fetch(src, dst):
        copy = pltpu.make_async_copy(src, dst, lsem.at[len(fetched)])
        fetched.append(copy)
        copy.start()
        return copy

    get_rows = fetch(srows_h, srows)
    get_k = fetch(K, kw.at[:, pl.ds(0, R)])
    get_l = fetch(L, wl.at[:, pl.ds(0, R)])
    own_half = pl.ds(pl.multiple_of(c * 512, 512), 512)
    get_w = fetch(wsh.at[:, own_half], wg.at[c, b, zl, a])
    get_q = fetch(Q, qv)
    get_small = [
        fetch(nbr_h, nbr), fetch(live_h, live), fetch(dec_h, dec), fetch(tgt_h, tgt), fetch(mult_h, mult)
    ]

    fa[:, CH:16] = jnp.zeros((MEMBERS, 16 - CH, R), F32)
    get_rows.wait()
    rows = iota((R, H), 0)
    to_right = (rows == srows[1:2, :]).astype(F32).astype(BF16)
    to_left = (rows == srows[0:1, :]).astype(F32).astype(BF16)
    oneh[:, 0:H] = to_right
    oneh[:, H:2 * H] = to_left
    get_k.wait()
    for m in range(M):
        snd_k[0, m] = dot(to_right, kw[m, 0:R], TN).astype(BF16)
        snd_k[1, m] = dot(to_left, kw[m, 0:R], TN).astype(BF16)
    get_l.wait()
    for m in range(M):
        snd_l[0, m] = dot(to_right, wl[m, 0:R], TN).astype(BF16)
        snd_l[1, m] = dot(to_left, wl[m, 0:R], TN).astype(BF16)
    get_w.wait()

    pl.semaphore_wait(barrier, len(partners))

    w1 = [send(wg.at[c, b, zl, a], wg.at[c, b, zl, a], peer_zl(k)) for k in (1, 2, 3)]
    def halo_keys():
        return [
            send(snd_k.at[0], kw.at[:, pl.ds(R, H)], right),
            send(snd_k.at[1], kw.at[:, pl.ds(R + H, H)], left),
        ]

    hk = halo_keys()

    def halo_latents():
        return [
            send(snd_l.at[0], wl.at[:, pl.ds(R, H)], right),
            send(snd_l.at[1], wl.at[:, pl.ds(R + H, H)], left),
        ]

    for copy in get_small:
        copy.wait()
    node_ids = nbr[...]
    row = iota((W, R), 0)
    wide_id = jnp.where(row < R, row + H, jnp.where(row < R + H, row - R, row))
    used = live[...]
    links = jnp.zeros((W, R), F32)
    for t in range(16):
        hit = jnp.where(used > t, node_ids[t:t + 1, :], -1) == wide_id
        links = links + jnp.where(hit, 1.0, 0.0)
    lk[:, 0:R] = links
    lk[:, R:2 * R] = links

    for k in range(3):
        w1[k].wait_recv()
    w2 = [send(wg.at[c, b, :, a], wg.at[c, b, :, a], peer_a(k)) for k in (1, 2, 3)]
    hl = halo_latents()

    get_q.wait()
    for m in range(M):
        for d in range(8):
            qt[m, d * 128:(d + 1) * 128, :] = qv[m, :, d * 128:(d + 1) * 128].T
            lt[m, d * 128:(d + 1) * 128, :] = wl[m, 0:R, d * 128:(d + 1) * 128].T
    slot, chan = iota((128, CHANNELS), 0), iota((128, CHANNELS), 1)
    place = ((slot % 16 < CH) & (chan == (slot // 16) * CH + slot % 16)).astype(F32).astype(BF16)
    slot_t, chan_t = iota((CHANNELS, 128), 1), iota((CHANNELS, 128), 0)
    place_t = ((slot_t % 16 < CH) & (chan_t == (slot_t // 16) * CH + slot_t % 16)).astype(F32).astype(BF16)
    decp[...] = dot(dec[...], place_t, TN).astype(BF16)
    decpt[...] = dot(place, dec[...]).astype(BF16)
    slot16, chan16 = iota((16, CHANNELS), 0), iota((16, CHANNELS), 1)
    own_place = ((slot16 < CH) & (chan16 == e * CH + slot16)).astype(F32)
    tgo[...] = lax.dot_general(
        own_place, tgt[...], (((1,), (0,)), ((), ())),
        precision=lax.Precision.HIGHEST, preferred_element_type=F32,
    )

    for k in range(3):
        w2[k].wait_recv()
    parts = [pl.ds(0, 256), pl.ds(256, 256)]
    w3 = [
        [send(wg.at[c, b, :, :, :, part], wg.at[c, b, :, :, :, part], peer_b(k)) for k in (1, 3, 2)]
        for part in parts
    ]
    wd = [send(wg.at[c, b], wg.at[c, b], sibling)]

    for k in range(2):
        hk[k].wait_recv()

    top = iota((128, R), 0) < 64

    def spread(block):
        zero = jnp.zeros_like(block)
        return jnp.concatenate([jnp.where(top, block, zero), jnp.where(top, zero, block)], axis=1)

    def folded(block):
        return jnp.where(top, block[:, 0:R], block[:, R:2 * R])

    def cols(p):
        return pl.ds(pl.multiple_of(p * 128, 128), 128)

    def weights_of(p, _):
        link = lk[...]
        for m in range(M):
            scores = dot(kw[m, :, cols(p)], spread(qt[m, cols(p), :])) * 0.125
            masked = jnp.where(link > 0, scores, -1e30)
            raised = link * jnp.exp(masked - jnp.max(masked, axis=0, keepdims=True))
            weight = raised * (1.0 / jnp.sum(raised, axis=0, keepdims=True))
            pf[m, p] = weight
            pb[m, p] = weight.astype(BF16)
        return 0

    lax.fori_loop(0, 4, weights_of, 0, unroll=2)
    for h, part in enumerate(parts):
        for i, k in enumerate((1, 3, 2)):
            w3[h][i].wait_recv()
            bk = (b + 4 - k) % 4
            wd.append(send(wg.at[c, bk, :, :, :, part], wg.at[c, bk, :, :, :, part], sibling))
    lax.fori_loop(4, PAIRS, weights_of, 0, unroll=2)
    for k in range(2):
        hl[k].wait_recv()
    for copy in wd:
        copy.wait_recv()

    for z_ in range(4):
        for y_ in range(4):
            for x_ in range(4):
                d = z_ * 256 + y_ * 64 + x_ * 16
                wf[d:d + 16, 0:512] = wg[0, x_, z_, y_]
                wf[d:d + 16, 512:1024] = wg[1, y_, z_, x_]

    def mix(m):
        def step(p, _):
            mixed = folded(dot(vv[m, :, cols(p)], pb[m, p], TN))
            outt[m, cols(p), :] = (lt[m, cols(p), :].astype(F32) + mixed).astype(BF16)
            return 0
        return step

    def values_of(q, _):
        block = pl.ds(pl.multiple_of(q * 256, 256), 256)
        both = dot(wl[...].reshape(M * W, D), wf[:, block]).astype(BF16)
        for m in range(M):
            vv[m, :, block] = both[m * W:(m + 1) * W]
        return 0

    lax.fori_loop(0, 4, values_of, 0)
    fx = []
    for m in range(M):
        lax.fori_loop(0, PAIRS, mix(m), 0, unroll=4)
        fs[m] = dot(decpt[...], outt[m]).reshape(8, 16, R)
        fa[2 * e + m] = fs[m, e]
        for k in range(1, 8):
            fx.append(send(fs.at[m, (e + k) % 8, pl.ds(0, CH)], fa.at[2 * e + m, pl.ds(0, CH)], peer_ens(k)))

    for m in range(M):
        for d in range(8):
            halo_t = wl[m, R:W, d * 128:(d + 1) * 128].T
            own_t = lt[m, d * 128:(d + 1) * 128, :]
            for i in range(8):
                g = d * 8 + i
                z_, y_, x_ = g // 16, (g // 4) % 4, g % 4
                r0 = (x_ * 16 + z_ * 4 + y_) * 16
                r1_ = (y_ * 16 + z_ * 4 + x_) * 16
                for h, r_ in ((0, r0), (1, r1_)):
                    wlt[h, m, r_:r_ + 16, 0:R] = own_t[i * 16:(i + 1) * 16]
                    wlt[h, m, r_:r_ + 16, R:W] = halo_t[i * 16:(i + 1) * 16]

    for copy in fx:
        copy.wait_recv()

    pair_norm = 1.0 / (MEMBERS * (MEMBERS - 1))

    def score(g, _):
        part = pl.ds(pl.multiple_of(g * 8, 8), 8)
        f = fa[:, part]
        shift = f - tgo[part][None]
        square = shift * shift + SMOOTH * SMOOTH
        inverse = lax.rsqrt(square)
        near = jnp.sum(square * inverse - SMOOTH, axis=0)
        pair_slope = jnp.zeros((MEMBERS, 8, R), F32)
        pair_total = jnp.zeros((8, R), F32)
        for k in range(1, 9):
            gap = f - jnp.concatenate([f[k:], f[:k]], axis=0)
            gap_square = gap * gap + SMOOTH * SMOOTH
            gap_inverse = lax.rsqrt(gap_square)
            radius = gap_square * gap_inverse - SMOOTH
            slope = gap * gap_inverse
            if k < 8:
                pair_total = pair_total + jnp.sum(radius, axis=0)
                back = jnp.concatenate([slope[MEMBERS - k:], slope[:MEMBERS - k]], axis=0)
                pair_slope = pair_slope + slope - back
            else:
                pair_total = pair_total + jnp.sum(radius[:8], axis=0)
                pair_slope = pair_slope + slope
        slf[:, part] = mult[0] * (shift * inverse * (1.0 / MEMBERS) - pair_slope * pair_norm)
        slot_id = iota((8, R), 0) + g * 8
        real = (slot_id < CH) & (slot_id + e * CH < CHANNELS)
        terms[g] = jnp.where(real, near * (1.0 / MEMBERS) - pair_total * pair_norm, 0.0)
        return 0

    lax.fori_loop(0, 2, score, 0)
    sl[...] = slf[...].astype(BF16)
    sx = [
        send(sl.at[pl.ds(2 * ((e + k) % 8), 2)], sr.at[e], peer_ens(k))
        for k in range(1, 8)
    ]
    sr[e] = sl[pl.ds(2 * e, 2)]
    lsend[0] = jnp.sum(terms[0] + terms[1], axis=0, keepdims=True)
    lrecv[0, zh] = lsend[0]
    l0 = [send(lsend.at[0], lrecv.at[0, zh], peer_zh(k)) for k in (1, 2, 3)]
    for copy in sx:
        copy.wait_recv()

    for m in range(M):
        dot_t[m] = dot(decp[...], sr[:, m].reshape(128, R)).astype(BF16)

    def value_grads(half, q):
        for i in range(2):
            p = half * 4 + q * 2 + i
            for m in range(M):
                dv[half, m, :, (q * 2 + i) * 128:(q * 2 + i + 1) * 128] = dot(
                    pb[m, p], spread(dot_t[m, cols(p), :]), NT
                ).astype(BF16)

    def weight_grad(half, q, block):
        block_rows = pl.ds(pl.multiple_of(block * 256, 256), 256)
        return dot(wlt[half, 0, block_rows, :], dv[half, 0, :, q * 256:(q + 1) * 256]) + dot(
            wlt[half, 1, block_rows, :], dv[half, 1, :, q * 256:(q + 1) * 256])

    def loss_step(stage, copies, mine, peers):
        for copy in copies:
            copy.wait_recv()
        got = lrecv[stage]
        if stage == 1:
            lsend[2] = got[0] + got[1]
        else:
            lsend[stage + 1] = (got[0] + got[1]) + (got[2] + got[3])
        lrecv[stage + 1, mine] = lsend[stage + 1]
        return [send(lsend.at[stage + 1], lrecv.at[stage + 1, mine], p) for p in peers]

    x1, x2, x3, x4, x5, x6 = ([None, None] for _ in range(6))
    for q in range(2):
        value_grads(1 - c, q)
        x1[q] = []
        for k in (1, 2, 3, 0):
            e1s[q, k] = weight_grad(1 - c, q, (b_other + k) % 4).astype(BF16)
            x1[q].append(send(e1s.at[q, k], e1r.at[q, k], sibling))
        value_grads(c, q)
        x2[q] = []
        for i, k in enumerate((1, 2, 3, 0)):
            total = weight_grad(c, q, (b + k) % 4)
            x1[q][i].wait_recv()
            total = total + e1r[q, k].astype(F32)
            if k:
                s1[q, k - 1] = total.astype(BF16)
                x2[q].append(send(s1.at[q, k - 1], r1.at[q, k - 1], peer_b(k)))
            else:
                a2[q] = total.reshape(4, 4, 16, 256)

    l1 = loss_step(0, l0, c, [sibling])

    def attention_grads(p, _):
        for m in range(M):
            grad_weight = dot(vv[m, :, cols(p)], spread(dot_t[m, cols(p), :])).astype(BF16).astype(F32)
            weight = pf[m, p]
            drift = jnp.sum(grad_weight * weight, axis=0, keepdims=True)
            grad_scores = (weight * (grad_weight - drift) * 0.125).astype(BF16)
            dk[m, :, cols(p)] = dot(grad_scores, spread(qt[m, cols(p), :]), NT).astype(BF16)
            grad_q = folded(dot(kw[m, :, cols(p)], grad_scores, TN))
            gq[m, :, cols(p)] = grad_q.astype(BF16).T
        return 0

    def second(q):
        for copy in x2[q]:
            copy.wait_recv()
        a2[q] = a2[q] + (
            r1[q, 0].astype(F32) + r1[q, 1].astype(F32) + r1[q, 2].astype(F32)
        ).reshape(4, 4, 16, 256)
        x3[q] = []
        for k in (1, 2, 3):
            s2[q, k - 1] = a2[q, :, (a + k) % 4].astype(BF16)
            x3[q].append(send(s2.at[q, k - 1], r2.at[q, k - 1], peer_a(k)))

    def third(q):
        for copy in x3[q]:
            copy.wait_recv()
        a3[q] = a2[q, :, a] + (r2[q, 0].astype(F32) + r2[q, 1].astype(F32) + r2[q, 2].astype(F32))
        x4[q] = []
        for k in (1, 2, 3):
            s3[q, k - 1] = a3[q, (zl + k) % 4].astype(BF16)
            x4[q].append(send(s3.at[q, k - 1], r3.at[q, k - 1], peer_zl(k)))

    def fourth(q):
        for copy in x4[q]:
            copy.wait_recv()
        s4[q] = (
            a3[q, zl] + (r3[q, 0].astype(F32) + r3[q, 1].astype(F32) + r3[q, 2].astype(F32))
        ).astype(BF16)
        r4[q, zh] = s4[q]
        x5[q] = [send(s4.at[q], r4.at[q, zh], peer_zh(k)) for k in (1, 2, 3)]

    def fifth(q):
        for copy in x5[q]:
            copy.wait_recv()
        fin[c, q] = (r4[q, 0].astype(F32) + r4[q, 1].astype(F32)) + (
            r4[q, 2].astype(F32) + r4[q, 3].astype(F32))
        x6[q] = send(fin.at[c, q], fin.at[c, q], sibling)

    def latent_grads(m):
        parts = [
            (dv[h, m, 0:R].astype(F32) + dot(oneh[...], rv[h, m])).astype(BF16) for h in range(2)
        ]
        out = dot(sr[:, m].reshape(128, R), decpt[...], TN).astype(BF16).astype(F32)
        out = out + dot(parts[0], wf[:, 0:512], NT) + dot(parts[1], wf[:, 512:1024], NT)
        gl[m] = out.astype(BF16)

    lax.fori_loop(0, 2, attention_grads, 0, unroll=2)
    l2 = loss_step(1, l1, b, [peer_b(k) for k in (1, 2, 3)])
    second(0)
    lax.fori_loop(2, 4, attention_grads, 0, unroll=2)
    second(1)
    hv = [
        send(dv.at[:, :, pl.ds(R + H, H)], rv.at[:, :, pl.ds(H, H)], right),
        send(dv.at[:, :, pl.ds(R, H)], rv.at[:, :, pl.ds(0, H)], left),
    ]
    lax.fori_loop(4, 6, attention_grads, 0, unroll=2)
    l3 = loss_step(2, l2, a, [peer_a(k) for k in (1, 2, 3)])
    third(0)
    lax.fori_loop(6, PAIRS, attention_grads, 0, unroll=2)
    third(1)
    hkb = [
        send(dk.at[:, pl.ds(R + H, H)], rk.at[:, pl.ds(H, H)], right),
        send(dk.at[:, pl.ds(R, H)], rk.at[:, pl.ds(0, H)], left),
    ]
    store = [fetch(gq, o_dq)]
    l4 = loss_step(3, l3, zl, [peer_zl(k) for k in (1, 2, 3)])
    fourth(0)
    fourth(1)
    for copy in hv:
        copy.wait_recv()
    latent_grads(0)
    latent_grads(1)
    store.append(fetch(gl, o_dl))
    l5 = loss_step(4, l4, c, [sibling])
    for copy in hkb:
        copy.wait_recv()
    for m in range(M):
        gk[m] = (dk[m, 0:R].astype(F32) + dot(oneh[...], rk[m])).astype(BF16)
    store.append(fetch(gk, o_dk))
    fifth(0)
    fifth(1)
    l5[0].wait_recv()
    o_loss[0, 0] = jnp.sum(lrecv[5, 0]) * (1.0 / (8192 * CHANNELS))
    for q in range(2):
        x6[q].wait_recv()
        for h in range(2):
            gw[:, h * 512 + q * 256:h * 512 + (q + 1) * 256] = fin[h, q]
    store.append(fetch(gw, o_dw))
    for copy in sent:
        copy.wait_send()
    for copy in store:
        copy.wait()


def hand_over(*refs):
    sources, results, held, sems = refs[:4], refs[4:8], refs[8:12], refs[12]
    arriving = [pltpu.make_async_copy(sources[i], held[i], sems.at[0, i]) for i in range(4)]
    leaving = [pltpu.make_async_copy(held[i], results[i], sems.at[1, i]) for i in range(4)]
    for copy in arriving:
        copy.start()
    for i in range(4):
        arriving[i].wait()
        leaving[i].start()
    for copy in leaving:
        copy.wait()


N_COPIES = 112


def body(latents, queries, attn_keys, value_weight, decoder, targets, send_rows, neighbours, live_slots, loss_multiplier):
    hbm = pl.BlockSpec(memory_space=pl.ANY)
    sm = pl.BlockSpec(memory_space=pltpu.SMEM)

    def buf(*shape, dtype=BF16):
        return pltpu.VMEM(shape, dtype)

    scratch = [
        buf(CHANNELS, D),
        buf(CHANNELS, R, dtype=F32),
        buf(2, H, dtype=jnp.int32),
        buf(16, R, dtype=jnp.int32),
        buf(1, R, dtype=jnp.int32),
        pltpu.SMEM((1,), F32),
        buf(M, R, D),
        buf(2, 4, 4, 4, 16, 512),
        buf(D, D),
        buf(M, W, D),
        buf(M, W, D),
        buf(M, D, R),
        buf(M, D, R),
        buf(2, M, D, W),
        buf(W, 2 * R, dtype=F32),
        buf(R, 2 * H),
        buf(2, M, H, D),
        buf(2, M, H, D),
        buf(D, 128),
        buf(128, D),
        buf(16, R, dtype=F32),
        buf(M, PAIRS, W, 2 * R, dtype=F32),
        buf(M, PAIRS, W, 2 * R),
        buf(M, W, D),
        buf(M, D, R),
        buf(M, 8, 16, R, dtype=F32),
        buf(MEMBERS, 16, R, dtype=F32),
        buf(MEMBERS, 16, R, dtype=F32),
        buf(2, 8, R, dtype=F32),
        buf(MEMBERS, 16, R),
        buf(8, M, 16, R),
        buf(M, D, R),
        buf(2, M, W, 512),
        buf(M, W, D),
        buf(2, M, 2 * H, 512),
        buf(M, 2 * H, D),
        buf(2, 4, 256, 256),
        buf(2, 4, 256, 256),
        buf(2, 3, 256, 256),
        buf(2, 3, 256, 256),
        buf(2, 4, 4, 16, 256, dtype=F32),
        buf(2, 3, 4, 16, 256),
        buf(2, 3, 4, 16, 256),
        buf(2, 4, 16, 256, dtype=F32),
        buf(2, 3, 16, 256),
        buf(2, 3, 16, 256),
        buf(2, 16, 256),
        buf(2, 4, 16, 256),
        buf(2, 2, 16, 256, dtype=F32),
        buf(6, 1, 128, dtype=F32),
        buf(6, 4, 1, 128, dtype=F32),
        buf(M, R, D),
        buf(M, R, D),
        buf(M, R, D),
        buf(16, D, dtype=F32),
        pltpu.SemaphoreType.DMA((N_COPIES,)),
        pltpu.SemaphoreType.DMA((N_COPIES,)),
        pltpu.SemaphoreType.DMA((16,)),
    ]
    loss, dl, dq, dk, dw = pl.pallas_call(
        kernel,
        out_shape=(
            jax.ShapeDtypeStruct((1, 1), F32),
            jax.ShapeDtypeStruct((M, R, D), BF16),
            jax.ShapeDtypeStruct((M, R, D), BF16),
            jax.ShapeDtypeStruct((M, R, D), BF16),
            jax.ShapeDtypeStruct((16, D), F32),
        ),
        in_specs=[hbm] * 10,
        out_specs=(sm, hbm, hbm, hbm, hbm),
        scratch_shapes=scratch,
        compiler_params=pltpu.CompilerParams(
            collective_id=0, has_side_effects=True, vmem_limit_bytes=56 * 1024 * 1024
        ),
    )(
        latents, queries, attn_keys, value_weight, decoder.T, targets, send_rows, neighbours.T,
        live_slots.reshape(1, R), loss_multiplier,
    )
    results = (dl, dq, dk, dw)
    dl, dq, dk, dw = pl.pallas_call(
        hand_over,
        out_shape=tuple(jax.ShapeDtypeStruct(r.shape, r.dtype) for r in results),
        in_specs=[hbm] * 4,
        out_specs=(hbm,) * 4,
        scratch_shapes=[pltpu.VMEM(r.shape, r.dtype) for r in results] + [pltpu.SemaphoreType.DMA((2, 4))],
    )(*results)
    return loss.reshape(1), dl, dq, dk, dw


def solution(mesh):
    rows = P("ens", "space", None)
    in_specs = (
        rows, rows, rows, P("space", None), P(), P(None, "space"), P(None, "space"),
        P("space", None), P("space"), P(),
    )
    out_specs = (P(), rows, rows, rows, P("space", None))
    return jax.shard_map(body, mesh=mesh, in_specs=in_specs, out_specs=out_specs, check_vma=False)
```

```python
import jax
import jax.numpy as jnp
from jax import lax
from jax.experimental import pallas as pl
from jax.experimental.pallas import tpu as pltpu
from jax.sharding import PartitionSpec as P

MESH = pl.DeviceIdType.MESH
F32 = jnp.float32
BF16 = jnp.bfloat16
M, R, D, H, W = 2, 128, 1024, 32, 192
PAIRS = 8
CH = 13
MEMBERS = 16
CHANNELS = 100
FAR_FIRST = (4, 3, 5, 2, 6, 1, 7)
SMOOTH = 0.1
NT = (((1,), (1,)), ((), ()))
TN = (((0,), (0,)), ((), ()))


def dot(a, b, dims=(((1,), (0,)), ((), ()))):
    return lax.dot_general(a, b, dims, preferred_element_type=F32)


def iota(shape, dim):
    return lax.broadcasted_iota(jnp.int32, shape, dim)


def kernel(
    L, Q, K, wsh, dec_h, tgt_h, srows_h, nbr_h, live_h, mult_h,
    o_loss, o_dl, o_dq, o_dk, o_dw,
    dec, tgt, srows, nbr, live, mult, qv,
    wg, wf, wl, kw, qt, lt, wlt, lk, oneh, snd_l, snd_k,
    decp, decpt, tgo, pf, pb, vv, outt, fs, fa, slf, terms, sl, sr, dot_t, dv, dk, rv, rk,
    e1s, e1r, s1, r1, a2, s2, r2, a3, s3, r3, s4, r4, fin, lsend, lrecv, gl, gq, gk, gw,
    ssem, rsem, lsem,
):
    e = lax.axis_index("ens")
    s = lax.axis_index("space")
    zh, c = e // 2, e % 2
    zl, y, x = s // 16, (s // 4) % 4, s % 4
    a = y * (1 - c) + x * c
    b = x * (1 - c) + y * c
    b_other = y * (1 - c) + x * c

    def at(e_, zl_, y_, x_):
        return (e_, zl_ * 16 + y_ * 4 + x_)

    sibling = (zh * 2 + 1 - c, s)

    def peer_a(k):
        return at(e, zl, (y + k * (1 - c)) % 4, (x + k * c) % 4)

    def peer_b(k):
        return at(e, zl, (y + k * c) % 4, (x + k * (1 - c)) % 4)

    def peer_zl(k):
        return at(e, (zl + k) % 4, y, x)

    def peer_zh(k):
        return (((zh + k) % 4) * 2 + c, s)

    def peer_ens(k):
        return ((e + k) % 8, s)

    right = (e, (s + 1) % 64)
    left = (e, (s + 63) % 64)

    barrier = pltpu.get_barrier_semaphore()
    partners = [peer_a(k) for k in (1, 2, 3)] + [peer_b(k) for k in (1, 2, 3)]
    partners += [peer_zl(k) for k in (1, 2, 3)] + [peer_ens(k) for k in range(1, 8)]
    partners += [right, left]
    for p in partners:
        pl.semaphore_signal(barrier, inc=1, device_id=p, device_id_type=MESH)

    sent = []
    count = [0]

    def send(src, dst, device):
        k = count[0]
        count[0] += 1
        copy = pltpu.make_async_remote_copy(
            src_ref=src, dst_ref=dst, send_sem=ssem.at[k], recv_sem=rsem.at[k],
            device_id=device, device_id_type=MESH,
        )
        copy.start()
        sent.append(copy)
        return copy

    fetched = []

    def fetch(src, dst):
        copy = pltpu.make_async_copy(src, dst, lsem.at[len(fetched)])
        fetched.append(copy)
        copy.start()
        return copy

    get_rows = fetch(srows_h, srows)
    get_k = fetch(K, kw.at[:, pl.ds(0, R)])
    get_l = fetch(L, wl.at[:, pl.ds(0, R)])
    own_half = pl.ds(pl.multiple_of(c * 512, 512), 512)
    get_w = fetch(wsh.at[:, own_half], wg.at[c, b, zl, a])
    get_q = fetch(Q, qv)
    get_small = [
        fetch(nbr_h, nbr), fetch(live_h, live), fetch(dec_h, dec), fetch(tgt_h, tgt), fetch(mult_h, mult)
    ]

    fa[:, CH:16] = jnp.zeros((MEMBERS, 16 - CH, R), F32)
    get_rows.wait()
    rows = iota((R, H), 0)
    to_right = (rows == srows[1:2, :]).astype(F32).astype(BF16)
    to_left = (rows == srows[0:1, :]).astype(F32).astype(BF16)
    oneh[:, 0:H] = to_right
    oneh[:, H:2 * H] = to_left
    get_k.wait()
    for m in range(M):
        snd_k[0, m] = dot(to_right, kw[m, 0:R], TN).astype(BF16)
        snd_k[1, m] = dot(to_left, kw[m, 0:R], TN).astype(BF16)
    get_l.wait()
    for m in range(M):
        snd_l[0, m] = dot(to_right, wl[m, 0:R], TN).astype(BF16)
        snd_l[1, m] = dot(to_left, wl[m, 0:R], TN).astype(BF16)
    get_w.wait()

    pl.semaphore_wait(barrier, len(partners))

    w1 = [send(wg.at[c, b, zl, a], wg.at[c, b, zl, a], peer_zl(k)) for k in (1, 2, 3)]
    def halo_keys():
        return [
            send(snd_k.at[0], kw.at[:, pl.ds(R, H)], right),
            send(snd_k.at[1], kw.at[:, pl.ds(R + H, H)], left),
        ]

    hk = halo_keys()

    def halo_latents():
        return [
            send(snd_l.at[0], wl.at[:, pl.ds(R, H)], right),
            send(snd_l.at[1], wl.at[:, pl.ds(R + H, H)], left),
        ]

    for copy in get_small:
        copy.wait()
    node_ids = nbr[...]
    row = iota((W, R), 0)
    wide_id = jnp.where(row < R, row + H, jnp.where(row < R + H, row - R, row))
    used = live[...]
    links = jnp.zeros((W, R), F32)
    for t in range(16):
        hit = jnp.where(used > t, node_ids[t:t + 1, :], -1) == wide_id
        links = links + jnp.where(hit, 1.0, 0.0)
    lk[:, 0:R] = links
    lk[:, R:2 * R] = links

    for k in range(3):
        w1[k].wait_recv()
    w2 = [send(wg.at[c, b, :, a], wg.at[c, b, :, a], peer_a(k)) for k in (1, 2, 3)]
    hl = halo_latents()

    get_q.wait()
    for m in range(M):
        for d in range(8):
            qt[m, d * 128:(d + 1) * 128, :] = qv[m, :, d * 128:(d + 1) * 128].T
            lt[m, d * 128:(d + 1) * 128, :] = wl[m, 0:R, d * 128:(d + 1) * 128].T
    slot, chan = iota((128, CHANNELS), 0), iota((128, CHANNELS), 1)
    place = ((slot % 16 < CH) & (chan == (slot // 16) * CH + slot % 16)).astype(F32).astype(BF16)
    slot_t, chan_t = iota((CHANNELS, 128), 1), iota((CHANNELS, 128), 0)
    place_t = ((slot_t % 16 < CH) & (chan_t == (slot_t // 16) * CH + slot_t % 16)).astype(F32).astype(BF16)
    decp[...] = dot(dec[...], place_t, TN).astype(BF16)
    decpt[...] = dot(place, dec[...]).astype(BF16)
    slot16, chan16 = iota((16, CHANNELS), 0), iota((16, CHANNELS), 1)
    own_place = ((slot16 < CH) & (chan16 == e * CH + slot16)).astype(F32)
    tgo[...] = lax.dot_general(
        own_place, tgt[...], (((1,), (0,)), ((), ())),
        precision=lax.Precision.HIGHEST, preferred_element_type=F32,
    )

    for k in range(3):
        w2[k].wait_recv()
    parts = [pl.ds(0, 256), pl.ds(256, 256)]
    w3 = [
        [send(wg.at[c, b, :, :, :, part], wg.at[c, b, :, :, :, part], peer_b(k)) for k in (2, 1, 3)]
        for part in parts
    ]
    wd = [send(wg.at[c, b], wg.at[c, b], sibling)]

    for k in range(2):
        hk[k].wait_recv()

    top = iota((128, R), 0) < 64

    def spread(block):
        zero = jnp.zeros_like(block)
        return jnp.concatenate([jnp.where(top, block, zero), jnp.where(top, zero, block)], axis=1)

    def folded(block):
        return jnp.where(top, block[:, 0:R], block[:, R:2 * R])

    def cols(p):
        return pl.ds(pl.multiple_of(p * 128, 128), 128)

    def weights_of(p, _):
        link = lk[...]
        for m in range(M):
            scores = dot(kw[m, :, cols(p)], spread(qt[m, cols(p), :])) * 0.125
            masked = jnp.where(link > 0, scores, -1e30)
            raised = link * jnp.exp(masked - jnp.max(masked, axis=0, keepdims=True))
            weight = raised * (1.0 / jnp.sum(raised, axis=0, keepdims=True))
            pf[m, p] = weight
            pb[m, p] = weight.astype(BF16)
        return 0

    lax.fori_loop(0, 4, weights_of, 0, unroll=2)
    for h, part in enumerate(parts):
        for i, k in enumerate((2, 1, 3)):
            w3[h][i].wait_recv()
            bk = (b + 4 - k) % 4
            wd.append(send(wg.at[c, bk, :, :, :, part], wg.at[c, bk, :, :, :, part], sibling))
    lax.fori_loop(4, PAIRS, weights_of, 0, unroll=2)
    for k in range(2):
        hl[k].wait_recv()
    for copy in wd:
        copy.wait_recv()

    for z_ in range(4):
        for y_ in range(4):
            for x_ in range(4):
                d = z_ * 256 + y_ * 64 + x_ * 16
                wf[d:d + 16, 0:512] = wg[0, x_, z_, y_]
                wf[d:d + 16, 512:1024] = wg[1, y_, z_, x_]

    def mix(m):
        def step(p, _):
            mixed = folded(dot(vv[m, :, cols(p)], pb[m, p], TN))
            outt[m, cols(p), :] = (lt[m, cols(p), :].astype(F32) + mixed).astype(BF16)
            return 0
        return step

    def values_of(q, _):
        block = pl.ds(pl.multiple_of(q * 256, 256), 256)
        both = dot(wl[...].reshape(M * W, D), wf[:, block]).astype(BF16)
        for m in range(M):
            vv[m, :, block] = both[m * W:(m + 1) * W]
        return 0

    lax.fori_loop(0, 4, values_of, 0)
    fx = []
    for m in range(M):
        lax.fori_loop(0, PAIRS, mix(m), 0, unroll=4)
        fs[m] = dot(decpt[...], outt[m]).reshape(8, 16, R)
        fa[2 * e + m] = fs[m, e]
        for k in FAR_FIRST:
            fx.append(send(fs.at[m, (e + k) % 8, pl.ds(0, CH)], fa.at[2 * e + m, pl.ds(0, CH)], peer_ens(k)))

    for m in range(M):
        for d in range(8):
            halo_t = wl[m, R:W, d * 128:(d + 1) * 128].T
            own_t = lt[m, d * 128:(d + 1) * 128, :]
            for i in range(8):
                g = d * 8 + i
                z_, y_, x_ = g // 16, (g // 4) % 4, g % 4
                r0 = (x_ * 16 + z_ * 4 + y_) * 16
                r1_ = (y_ * 16 + z_ * 4 + x_) * 16
                for h, r_ in ((0, r0), (1, r1_)):
                    wlt[h, m, r_:r_ + 16, 0:R] = own_t[i * 16:(i + 1) * 16]
                    wlt[h, m, r_:r_ + 16, R:W] = halo_t[i * 16:(i + 1) * 16]

    for copy in fx:
        copy.wait_recv()

    pair_norm = 1.0 / (MEMBERS * (MEMBERS - 1))

    def score(g, _):
        part = pl.ds(pl.multiple_of(g * 8, 8), 8)
        f = fa[:, part]
        shift = f - tgo[part][None]
        square = shift * shift + SMOOTH * SMOOTH
        inverse = lax.rsqrt(square)
        near = jnp.sum(square * inverse - SMOOTH, axis=0)
        pair_slope = jnp.zeros((MEMBERS, 8, R), F32)
        pair_total = jnp.zeros((8, R), F32)
        for k in range(1, 9):
            gap = f - jnp.concatenate([f[k:], f[:k]], axis=0)
            gap_square = gap * gap + SMOOTH * SMOOTH
            gap_inverse = lax.rsqrt(gap_square)
            radius = gap_square * gap_inverse - SMOOTH
            slope = gap * gap_inverse
            if k < 8:
                pair_total = pair_total + jnp.sum(radius, axis=0)
                back = jnp.concatenate([slope[MEMBERS - k:], slope[:MEMBERS - k]], axis=0)
                pair_slope = pair_slope + slope - back
            else:
                pair_total = pair_total + jnp.sum(radius[:8], axis=0)
                pair_slope = pair_slope + slope
        slf[:, part] = mult[0] * (shift * inverse * (1.0 / MEMBERS) - pair_slope * pair_norm)
        slot_id = iota((8, R), 0) + g * 8
        real = (slot_id < CH) & (slot_id + e * CH < CHANNELS)
        terms[g] = jnp.where(real, near * (1.0 / MEMBERS) - pair_total * pair_norm, 0.0)
        return 0

    lax.fori_loop(0, 2, score, 0)
    sl[...] = slf[...].astype(BF16)
    sx = [
        send(sl.at[pl.ds(2 * ((e + k) % 8), 2)], sr.at[e], peer_ens(k))
        for k in FAR_FIRST
    ]
    sr[e] = sl[pl.ds(2 * e, 2)]
    lsend[0] = jnp.sum(terms[0] + terms[1], axis=0, keepdims=True)
    lrecv[0, zh] = lsend[0]
    l0 = [send(lsend.at[0], lrecv.at[0, zh], peer_zh(k)) for k in (2, 1, 3)]
    for copy in sx:
        copy.wait_recv()

    for m in range(M):
        dot_t[m] = dot(decp[...], sr[:, m].reshape(128, R)).astype(BF16)

    def value_grads(half, q):
        for i in range(2):
            p = half * 4 + q * 2 + i
            for m in range(M):
                dv[half, m, :, (q * 2 + i) * 128:(q * 2 + i + 1) * 128] = dot(
                    pb[m, p], spread(dot_t[m, cols(p), :]), NT
                ).astype(BF16)

    def weight_grad(half, q, block):
        block_rows = pl.ds(pl.multiple_of(block * 256, 256), 256)
        return dot(wlt[half, 0, block_rows, :], dv[half, 0, :, q * 256:(q + 1) * 256]) + dot(
            wlt[half, 1, block_rows, :], dv[half, 1, :, q * 256:(q + 1) * 256])

    def loss_step(stage, copies, mine, peers):
        for copy in copies:
            copy.wait_recv()
        got = lrecv[stage]
        if stage == 1:
            lsend[2] = got[0] + got[1]
        else:
            lsend[stage + 1] = (got[0] + got[1]) + (got[2] + got[3])
        lrecv[stage + 1, mine] = lsend[stage + 1]
        return [send(lsend.at[stage + 1], lrecv.at[stage + 1, mine], p) for p in peers]

    x1, x2, x3, x4, x5, x6 = ([None, None] for _ in range(6))
    for q in range(2):
        value_grads(1 - c, q)
        x1[q] = []
        for k in (2, 1, 3, 0):
            e1s[q, k] = weight_grad(1 - c, q, (b_other + k) % 4).astype(BF16)
            x1[q].append(send(e1s.at[q, k], e1r.at[q, k], sibling))
        value_grads(c, q)
        x2[q] = []
        for i, k in enumerate((2, 1, 3, 0)):
            total = weight_grad(c, q, (b + k) % 4)
            x1[q][i].wait_recv()
            total = total + e1r[q, k].astype(F32)
            if k:
                s1[q, k - 1] = total.astype(BF16)
                x2[q].append(send(s1.at[q, k - 1], r1.at[q, k - 1], peer_b(k)))
            else:
                a2[q] = total.reshape(4, 4, 16, 256)

    l1 = loss_step(0, l0, c, [sibling])

    def attention_grads(p, _):
        for m in range(M):
            grad_weight = dot(vv[m, :, cols(p)], spread(dot_t[m, cols(p), :])).astype(BF16).astype(F32)
            weight = pf[m, p]
            drift = jnp.sum(grad_weight * weight, axis=0, keepdims=True)
            grad_scores = (weight * (grad_weight - drift) * 0.125).astype(BF16)
            dk[m, :, cols(p)] = dot(grad_scores, spread(qt[m, cols(p), :]), NT).astype(BF16)
            grad_q = folded(dot(kw[m, :, cols(p)], grad_scores, TN))
            gq[m, :, cols(p)] = grad_q.astype(BF16).T
        return 0

    def second(q):
        for copy in x2[q]:
            copy.wait_recv()
        a2[q] = a2[q] + (
            r1[q, 0].astype(F32) + r1[q, 1].astype(F32) + r1[q, 2].astype(F32)
        ).reshape(4, 4, 16, 256)
        x3[q] = []
        for k in (2, 1, 3):
            s2[q, k - 1] = a2[q, :, (a + k) % 4].astype(BF16)
            x3[q].append(send(s2.at[q, k - 1], r2.at[q, k - 1], peer_a(k)))

    def third(q):
        for copy in x3[q]:
            copy.wait_recv()
        a3[q] = a2[q, :, a] + (r2[q, 0].astype(F32) + r2[q, 1].astype(F32) + r2[q, 2].astype(F32))
        x4[q] = []
        for k in (1, 2, 3):
            s3[q, k - 1] = a3[q, (zl + k) % 4].astype(BF16)
            x4[q].append(send(s3.at[q, k - 1], r3.at[q, k - 1], peer_zl(k)))

    def fourth(q):
        for copy in x4[q]:
            copy.wait_recv()
        s4[q] = (
            a3[q, zl] + (r3[q, 0].astype(F32) + r3[q, 1].astype(F32) + r3[q, 2].astype(F32))
        ).astype(BF16)
        r4[q, zh] = s4[q]
        x5[q] = [send(s4.at[q], r4.at[q, zh], peer_zh(k)) for k in (2, 1, 3)]

    def fifth(q):
        for copy in x5[q]:
            copy.wait_recv()
        fin[c, q] = (r4[q, 0].astype(F32) + r4[q, 1].astype(F32)) + (
            r4[q, 2].astype(F32) + r4[q, 3].astype(F32))
        x6[q] = send(fin.at[c, q], fin.at[c, q], sibling)

    def latent_grads(m):
        parts = [
            (dv[h, m, 0:R].astype(F32) + dot(oneh[...], rv[h, m])).astype(BF16) for h in range(2)
        ]
        out = dot(sr[:, m].reshape(128, R), decpt[...], TN).astype(BF16).astype(F32)
        out = out + dot(parts[0], wf[:, 0:512], NT) + dot(parts[1], wf[:, 512:1024], NT)
        gl[m] = out.astype(BF16)

    lax.fori_loop(0, 2, attention_grads, 0, unroll=2)
    l2 = loss_step(1, l1, b, [peer_b(k) for k in (1, 2, 3)])
    second(0)
    lax.fori_loop(2, 4, attention_grads, 0, unroll=2)
    second(1)
    hv = [
        send(dv.at[:, :, pl.ds(R + H, H)], rv.at[:, :, pl.ds(H, H)], right),
        send(dv.at[:, :, pl.ds(R, H)], rv.at[:, :, pl.ds(0, H)], left),
    ]
    lax.fori_loop(4, 6, attention_grads, 0, unroll=2)
    l3 = loss_step(2, l2, a, [peer_a(k) for k in (1, 2, 3)])
    third(0)
    lax.fori_loop(6, PAIRS, attention_grads, 0, unroll=2)
    third(1)
    hkb = [
        send(dk.at[:, pl.ds(R + H, H)], rk.at[:, pl.ds(H, H)], right),
        send(dk.at[:, pl.ds(R, H)], rk.at[:, pl.ds(0, H)], left),
    ]
    store = [fetch(gq, o_dq)]
    l4 = loss_step(3, l3, zl, [peer_zl(k) for k in (1, 2, 3)])
    fourth(0)
    fourth(1)
    for copy in hv:
        copy.wait_recv()
    latent_grads(0)
    latent_grads(1)
    store.append(fetch(gl, o_dl))
    l5 = loss_step(4, l4, c, [sibling])
    for copy in hkb:
        copy.wait_recv()
    for m in range(M):
        gk[m] = (dk[m, 0:R].astype(F32) + dot(oneh[...], rk[m])).astype(BF16)
    store.append(fetch(gk, o_dk))
    fifth(0)
    fifth(1)
    l5[0].wait_recv()
    o_loss[0, 0] = jnp.sum(lrecv[5, 0]) * (1.0 / (8192 * CHANNELS))
    for q in range(2):
        x6[q].wait_recv()
        for h in range(2):
            gw[:, h * 512 + q * 256:h * 512 + (q + 1) * 256] = fin[h, q]
    store.append(fetch(gw, o_dw))
    for copy in sent:
        copy.wait_send()
    for copy in store:
        copy.wait()


def hand_over(*refs):
    sources, results, held, sems = refs[:4], refs[4:8], refs[8:12], refs[12]
    arriving = [pltpu.make_async_copy(sources[i], held[i], sems.at[0, i]) for i in range(4)]
    leaving = [pltpu.make_async_copy(held[i], results[i], sems.at[1, i]) for i in range(4)]
    for copy in arriving:
        copy.start()
    for i in range(4):
        arriving[i].wait()
        leaving[i].start()
    for copy in leaving:
        copy.wait()


N_COPIES = 112


def body(latents, queries, attn_keys, value_weight, decoder, targets, send_rows, neighbours, live_slots, loss_multiplier):
    hbm = pl.BlockSpec(memory_space=pl.ANY)
    sm = pl.BlockSpec(memory_space=pltpu.SMEM)

    def buf(*shape, dtype=BF16):
        return pltpu.VMEM(shape, dtype)

    scratch = [
        buf(CHANNELS, D),
        buf(CHANNELS, R, dtype=F32),
        buf(2, H, dtype=jnp.int32),
        buf(16, R, dtype=jnp.int32),
        buf(1, R, dtype=jnp.int32),
        pltpu.SMEM((1,), F32),
        buf(M, R, D),
        buf(2, 4, 4, 4, 16, 512),
        buf(D, D),
        buf(M, W, D),
        buf(M, W, D),
        buf(M, D, R),
        buf(M, D, R),
        buf(2, M, D, W),
        buf(W, 2 * R, dtype=F32),
        buf(R, 2 * H),
        buf(2, M, H, D),
        buf(2, M, H, D),
        buf(D, 128),
        buf(128, D),
        buf(16, R, dtype=F32),
        buf(M, PAIRS, W, 2 * R, dtype=F32),
        buf(M, PAIRS, W, 2 * R),
        buf(M, W, D),
        buf(M, D, R),
        buf(M, 8, 16, R, dtype=F32),
        buf(MEMBERS, 16, R, dtype=F32),
        buf(MEMBERS, 16, R, dtype=F32),
        buf(2, 8, R, dtype=F32),
        buf(MEMBERS, 16, R),
        buf(8, M, 16, R),
        buf(M, D, R),
        buf(2, M, W, 512),
        buf(M, W, D),
        buf(2, M, 2 * H, 512),
        buf(M, 2 * H, D),
        buf(2, 4, 256, 256),
        buf(2, 4, 256, 256),
        buf(2, 3, 256, 256),
        buf(2, 3, 256, 256),
        buf(2, 4, 4, 16, 256, dtype=F32),
        buf(2, 3, 4, 16, 256),
        buf(2, 3, 4, 16, 256),
        buf(2, 4, 16, 256, dtype=F32),
        buf(2, 3, 16, 256),
        buf(2, 3, 16, 256),
        buf(2, 16, 256),
        buf(2, 4, 16, 256),
        buf(2, 2, 16, 256, dtype=F32),
        buf(6, 1, 128, dtype=F32),
        buf(6, 4, 1, 128, dtype=F32),
        buf(M, R, D),
        buf(M, R, D),
        buf(M, R, D),
        buf(16, D, dtype=F32),
        pltpu.SemaphoreType.DMA((N_COPIES,)),
        pltpu.SemaphoreType.DMA((N_COPIES,)),
        pltpu.SemaphoreType.DMA((16,)),
    ]
    loss, dl, dq, dk, dw = pl.pallas_call(
        kernel,
        out_shape=(
            jax.ShapeDtypeStruct((1, 1), F32),
            jax.ShapeDtypeStruct((M, R, D), BF16),
            jax.ShapeDtypeStruct((M, R, D), BF16),
            jax.ShapeDtypeStruct((M, R, D), BF16),
            jax.ShapeDtypeStruct((16, D), F32),
        ),
        in_specs=[hbm] * 10,
        out_specs=(sm, hbm, hbm, hbm, hbm),
        scratch_shapes=scratch,
        compiler_params=pltpu.CompilerParams(
            collective_id=0, has_side_effects=True, vmem_limit_bytes=56 * 1024 * 1024
        ),
    )(
        latents, queries, attn_keys, value_weight, decoder.T, targets, send_rows, neighbours.T,
        live_slots.reshape(1, R), loss_multiplier,
    )
    results = (dl, dq, dk, dw)
    dl, dq, dk, dw = pl.pallas_call(
        hand_over,
        out_shape=tuple(jax.ShapeDtypeStruct(r.shape, r.dtype) for r in results),
        in_specs=[hbm] * 4,
        out_specs=(hbm,) * 4,
        scratch_shapes=[pltpu.VMEM(r.shape, r.dtype) for r in results] + [pltpu.SemaphoreType.DMA((2, 4))],
    )(*results)
    return loss.reshape(1), dl, dq, dk, dw


def solution(mesh):
    rows = P("ens", "space", None)
    in_specs = (
        rows, rows, rows, P("space", None), P(), P(None, "space"), P(None, "space"),
        P("space", None), P("space"), P(),
    )
    out_specs = (P(), rows, rows, rows, P("space", None))
    return jax.shard_map(body, mesh=mesh, in_specs=in_specs, out_specs=out_specs, check_vma=False)
```
